256 devices in a mesh: space: 128 (over x, z, y), chan: 2 (over core).
Axes of the slice: x: 4, y: 4, z: 8, core: 2. Of those that a mesh axis runs over, the one named last changes fastest.
Arguments:
- features: bfloat16 [1024, 512, 128], P('space', None, 'chan'), may hold values from -6 to 6
- heights: int32 [1024, 64], P('space'), may hold values from 0 to 8
- neighbours: int32 [128, 26], P('space'), may hold values from -1 to 127, as said below
- w_conv: bfloat16 [27, 128, 128], replicated, may hold values from -0.109375 to 0.109375
- w_down: bfloat16 [8, 128, 256], replicated, may hold values from -0.1875 to 0.1875
- cotangent: bfloat16 [128, 512, 256], P('space'), may hold values from -12 to 12
Outputs:
- coarse: bfloat16 [128, 512, 256], P('space', None, 'chan')
- grad_conv: float32 [27, 128, 128], P(None, 'chan')
- grad_down: float32 [8, 128, 256], P(None, None, 'chan')
- grad_features: bfloat16 [1024, 512, 128], P('space', None, 'chan')
The draws below stay inside these ranges and needn't reach their ends.
Inputs may be any that keep to these rules, and one draw needn't show every extreme that they name: neighbours[s, k] is the block at offset d_k from block s (the 26 offsets of the finite set (-1,0,1)^3 without the anchor, lexicographic in (x, y, z)), or -1 where no block is there; if neighbours[s, k] = q then neighbours[q, 25 - k] = s; distinct offsets name distinct blocks; blocks lie on a strip two positions wide and two high and are numbered in order of x, then y, then z, so that every neighbour q of s has 1 <= |q - s| <= 7.
All inputs are finite; a program needn't handle non-finite values.
Results may differ from the reference program's by a relative error of at most 0.005.
Values may be sent and summed in bfloat16 or wider, within the bound.
A program may use at most 320 MiB of HBM per device.

```python
import jax
import jax.numpy as jnp
from jax import lax

C = 128
CO = 256
BLOCKS = 128
BRICKS = 1024
FOOTX = 64


def draw_neighbours(key, part):
    key = jax.random.fold_in(key, 11)
    total = 2 * BLOCKS
    places = jnp.arange(total, dtype=jnp.int32)
    noise = jax.random.randint(key, (total,), 0, 1 << 20, dtype=jnp.int32)
    scores = noise * total + places
    chosen = jnp.argsort(scores)[:BLOCKS].astype(jnp.int32)
    cells = jnp.sort(chosen).astype(jnp.int32)
    coord_x = places // 4
    coord_y = places // 2 % 2
    coord_z = places % 2
    table = jnp.full((total,), -1, jnp.int32).at[cells].set(jnp.arange(BLOCKS, dtype=jnp.int32))
    result = []
    for along_x in (-1, 0, 1):
        for along_y in (-1, 0, 1):
            for along_z in (-1, 0, 1):
                if (along_x, along_y, along_z) != (0, 0, 0):
                    next_x = coord_x[cells] + along_x
                    next_y = coord_y[cells] + along_y
                    next_z = coord_z[cells] + along_z
                    inside = (next_x >= 0) & (next_x < FOOTX) & (next_y >= 0) & (next_y < 2) & (next_z >= 0) & (next_z < 2)
                    place = (jnp.clip(next_x, 0, FOOTX - 1) * 2 + jnp.clip(next_y, 0, 1)) * 2 + jnp.clip(next_z, 0, 1)
                    result.append(jnp.where(inside, table[place], -1))
    return jnp.stack(result, axis=1).astype(jnp.int32)


def plant(array, rng, least, high):
    index_at = [jax.random.randint(jax.random.fold_in(rng, axis), (), 0, length) for axis, length in enumerate(array.shape)]
    widest = array.shape.index(max(array.shape))
    beside = index_at[:widest] + [(index_at[widest] + 1) % array.shape[widest]] + index_at[widest + 1:]
    return array.at[tuple(index_at)].set(least).at[tuple(beside)].set(high)


def level_of(stream_key, shape, pieces, low, high):
    def one(axis_at, parts):
        draws = jax.random.uniform(jax.random.fold_in(jax.random.fold_in(stream_key, 6), axis_at), (parts,), jnp.float32, low / len(pieces), high / len(pieces))
        return jnp.repeat(jnp.exp(draws), shape[axis_at] // parts).reshape((-1,) + (1,) * (len(shape) - axis_at - 1))

    gain = one(*pieces[0])
    for cut in pieces[1:]:
        gain = gain * one(*cut)
    return gain


def normal_values(rng, extent, width, reach, cuts=(), held_as=jnp.bfloat16):
    values = width * jax.random.normal(rng, extent, jnp.float32)
    if cuts:
        values = values * level_of(rng, extent, cuts, -0.22, 0.18)
    return jnp.clip(values, -reach, reach).astype(held_as)


def setup_inputs(seed: int = 0) -> dict:
    splits = jax.random.split(jax.random.key(seed), 7)
    features = normal_values(splits[0], (BRICKS, 512, C), 1.0, 6.0, ((0, 128), (2, 2)))
    heights = plant(jax.random.randint(splits[1], (BRICKS, 64), 0, 9), jax.random.fold_in(splits[1], 1), 0, 8).astype(jnp.int32)
    neighbours = draw_neighbours(jax.random.fold_in(splits[6], 71), 0)
    w_conv = normal_values(splits[3], (27, C, C), (27 * C) ** -0.5, 0.109375)
    w_down = normal_values(splits[4], (8, C, CO), (8 * C) ** -0.5, 0.1875)
    cotangent = normal_values(splits[5], (BLOCKS, 512, CO), 2.0, 12.0, ((0, 128),))
    return {"features": features, "heights": heights, "neighbours": neighbours, "w_conv": w_conv, "w_down": w_down, "cotangent": cotangent}


OFFSETS = [(along_x, along_y, along_z) for along_x in (-1, 0, 1) for along_y in (-1, 0, 1) for along_z in (-1, 0, 1)]
DIRECTIONS = [offset for offset in OFFSETS if offset != (0, 0, 0)]


def blocks_of(bricks):
    count_blocks = bricks.shape[0] // 8
    channels = bricks.shape[-1]
    shaped = bricks.reshape(count_blocks, 2, 2, 2, 8, 8, 8, channels)
    return shaped.transpose(0, 3, 4, 2, 5, 1, 6, 7).reshape(count_blocks, 16, 16, 16, channels)


def bricks_of(volumes):
    count_blocks = volumes.shape[0]
    channels = volumes.shape[-1]
    shaped = volumes.reshape(count_blocks, 2, 8, 2, 8, 2, 8, channels)
    return shaped.transpose(0, 5, 3, 1, 2, 4, 6, 7).reshape(count_blocks * 8, 512, channels)


def pad_all(volumes, neighbours):
    padded = jnp.pad(volumes, ((0, 0), (1, 1), (1, 1), (1, 1), (0, 0)))
    for number, offset in enumerate(DIRECTIONS):
        source = tuple(slice(0, 1) if step_one == 1 else slice(15, 16) if step_one == -1 else slice(0, 16) for step_one in offset)
        target = tuple(slice(17, 18) if step_one == 1 else slice(0, 1) if step_one == -1 else slice(1, 17) for step_one in offset)
        other = neighbours[:, number]
        window = volumes[jnp.maximum(other, 0).astype(jnp.int32)][(slice(None),) + source]
        window = window * (other >= 0).astype(volumes.dtype)[:, None, None, None, None]
        padded = padded.at[(slice(None),) + target].set(window)
    return padded


def conv_block(padded, weights, sign):
    inputs = padded.shape[-1]
    summed = jnp.zeros((4096, weights.shape[-1]), jnp.float32)
    for number, (along_x, along_y, along_z) in enumerate(OFFSETS):
        window = padded[1 + sign * along_x:17 + sign * along_x, 1 + sign * along_y:17 + sign * along_y, 1 + sign * along_z:17 + sign * along_z]
        summed = summed + jnp.dot(window.reshape(4096, inputs), weights[number], preferred_element_type=jnp.float32)
    return summed


def tap_sums(padded, grad_rows):
    inputs = padded.shape[-1]
    result = []
    for along_x, along_y, along_z in OFFSETS:
        window = padded[1 + along_x:17 + along_x, 1 + along_y:17 + along_y, 1 + along_z:17 + along_z]
        result.append(jnp.dot(window.reshape(4096, inputs).T, grad_rows, preferred_element_type=jnp.float32))
    return jnp.stack(result)


def reference(features, heights, neighbours, w_conv, w_down, cotangent):
    levels = jnp.arange(8, dtype=jnp.int32)
    active = (levels[None, None, :] < heights[:, :, None]).astype(jnp.bfloat16).reshape(BRICKS, 512, 1)
    volumes = blocks_of(features * active)
    masks = blocks_of(active)
    padded = pad_all(volumes, neighbours)
    flat_down = w_down.reshape(8 * C, CO)

    def forward(carry, inputs):
        grad_conv, grad_down = carry
        pad_one, mask_one, upstream = inputs
        mask_rows = mask_one.reshape(4096, 1).astype(jnp.float32)
        pre = conv_block(pad_one, w_conv, 1) * mask_rows
        hidden = jax.nn.silu(pre).astype(jnp.bfloat16)
        patches = hidden.reshape(8, 2, 8, 2, 8, 2, C).transpose(0, 2, 4, 1, 3, 5, 6).reshape(512, 8 * C)
        coarse_one = jnp.dot(patches, flat_down, preferred_element_type=jnp.float32).astype(jnp.bfloat16)
        grad_down = grad_down + jnp.dot(patches.T, upstream, preferred_element_type=jnp.float32)
        grad_patches = jnp.dot(upstream, flat_down.T, preferred_element_type=jnp.float32)
        grad_hidden = grad_patches.reshape(8, 8, 8, 2, 2, 2, C).transpose(0, 3, 1, 4, 2, 5, 6).reshape(4096, C)
        sigmoid_pre = jax.nn.sigmoid(pre)
        grad_pre = (grad_hidden * sigmoid_pre * (1.0 + pre * (1.0 - sigmoid_pre)) * mask_rows).astype(jnp.bfloat16)
        grad_conv = grad_conv + tap_sums(pad_one, grad_pre)
        return (grad_conv, grad_down), (coarse_one, grad_pre.reshape(16, 16, 16, C))

    initial = (jnp.zeros((27, C, C), jnp.float32), jnp.zeros((8 * C, CO), jnp.float32))
    (grad_conv, grad_down), (coarse, grad_pre) = lax.scan(forward, initial, (padded, masks, cotangent))
    grad_padded = pad_all(grad_pre, neighbours)
    back_weights = w_conv.transpose(0, 2, 1)

    def backward(inputs):
        pad_one, mask_one = inputs
        rows = conv_block(pad_one, back_weights, -1) * mask_one.reshape(4096, 1).astype(jnp.float32)
        return rows.astype(jnp.bfloat16).reshape(16, 16, 16, C)

    grad_input = lax.map(backward, (grad_padded, masks))
    grad_features = bricks_of(grad_input)
    return coarse, grad_conv / BLOCKS, (grad_down / BLOCKS).reshape(8, C, CO), grad_features
```

```python
import jax
import jax.numpy as jnp
from jax import lax
from jax.experimental import pallas as pl
from jax.experimental.pallas import tpu as pltpu
from jax.sharding import PartitionSpec as P

MESH = pl.DeviceIdType.MESH
F32 = jnp.float32
BF16 = jnp.bfloat16
MID = slice(128, 256)
XS, ZS, YS = 4, 8, 4
BLOCKS = XS * ZS * YS


def dot(a, b):
    return jnp.dot(a, b, preferred_element_type=F32)


def dot_t(a, b):
    return lax.dot_general(a, b, (((1,), (1,)), ((), ())), preferred_element_type=F32)


def kernel(
    heights, near, feat, w_conv, w_down, cot,
    coarse, g_conv, g_down, g_feat,
    pad, gpad, mask, up, vol, cat, hid, patches, turned, w_back, out_bricks,
    shift_a, shift_b, margin,
    faces, edges, y_low_0, y_low_1, y_high_0, y_high_1, z_low, z_high, far_0, far_1, far_edge_0, far_edge_1,
    coarse_st, down_st, down_in, conv_st, conv_in,
    c_bf, c_in, c_mid, c_in2, c_tot, c_all,
    d_bf, d_in, d_mid, d_in2, d_tot, d_mix, d_all,
    halo_s, halo_r, pair_s, pair_r,
    c1_s, c1_r, c2_s, c2_r, c3_s, c3_r, c4_s, c4_r,
    d1_s, d1_r, d2_s, d2_r, d3_s, d3_r, d4_s, d4_r,
):
    y_low, y_high = (y_low_0, y_low_1), (y_high_0, y_high_1)
    far, far_edge = (far_0, far_1), (far_edge_0, far_edge_1)
    s = lax.axis_index("space")
    m = lax.axis_index("chan")
    other = 1 - m
    sign = 2 * m - 1
    my_y = s % YS
    my_z = s // YS % ZS
    my_x = s // (YS * ZS)
    plane = my_x * YS + my_y
    wrap = lambda index: (index + 2 * BLOCKS) % BLOCKS
    plane_steps = [(a, b) for a in range(XS) for b in range(YS) if (a, b) != (0, 0)]

    def plane_peer(step):
        x, y = (my_x + step[0]) % XS, (my_y + step[1]) % YS
        return x * YS + y, ((x * ZS + my_z) * YS + y, m)

    def line_peer(step):
        z = (my_z + step) % ZS
        return z, ((my_x * ZS + z) * YS + my_y, m)

    def remote(src, dst, send, recv, device):
        return pltpu.make_async_remote_copy(
            src_ref=src, dst_ref=dst, send_sem=send, recv_sem=recv, device_id=device, device_id_type=MESH
        )

    barrier = pltpu.get_barrier_semaphore()
    greeted = [(s, other)]
    for d in (1, 2, 3):
        for e in (d, -d):
            greeted += [(wrap(s + e), m), (wrap(s + e), other)]
    greeted += [(wrap(s + sign * j), other) for j in (4, 5, 6, 7)]
    greeted += [plane_peer(step)[1] for step in plane_steps]
    greeted += [line_peer(step)[1] for step in range(1, ZS)]
    for device in greeted:
        pl.semaphore_signal(barrier, inc=1, device_id=device, device_id_type=MESH)

    levels = lax.broadcasted_iota(jnp.int32, (8, 128), 0)

    def mask_plane(x, _):
        for y in range(16):
            for z in range(2):
                height = heights[m + 2 * (y // 8) + 4 * z, x * 8 + y % 8]
                mask[x, y, 8 * z:8 * z + 8, :] = jnp.where(levels < height, 1.0, 0.0)
        return 0

    lax.fori_loop(0, 8, mask_plane, 0)
    own_cot = cot[pl.ds(pl.multiple_of(m * 256, 256), 256), :]

    def upstream(t, _):
        rows = w_down[pl.ds(pl.multiple_of(t * 256, 256), 256), :]
        got = dot_t(own_cot, rows)
        for z in range(2):
            part = got[:, 128 * z:128 * z + 128].reshape(4, 8, 8, 128)
            for x in range(4):
                up[x, t // 2, :, t % 2, pl.ds(z, 8, stride=2), :] = part[x]
        return 0

    lax.fori_loop(0, 4, upstream, 0)

    def turn_back(tap, _):
        w_back[tap] = w_conv[26 - tap].astype(F32).T.astype(BF16)
        return 0

    lax.fori_loop(0, 27, turn_back, 0)

    pl.semaphore_wait(barrier, len(greeted))

    pair = (s, other)
    own_rows = pl.ds(pl.multiple_of(m * 64, 64), 64)
    other_rows = pl.ds(pl.multiple_of(other * 64, 64), 64)
    swap = remote(feat.at[:, other], cat.at[:, own_rows, :], pair_s.at[0], pair_r.at[0], pair)
    swap.start()
    cat[:, own_rows, :] = feat[:, m]
    swap.wait()

    for oy in range(2):
        for half in range(2):
            columns = slice(256 * half, 256 * half + 256)
            low = cat[oy, :, columns].astype(F32).T.reshape(4, 8, 8, 128)
            high = cat[oy + 2, :, columns].astype(F32).T.reshape(4, 8, 8, 128)
            both = jnp.concatenate([low, high], axis=2)
            at = slice(4 * half, 4 * half + 4)
            both = both * mask[at, 8 * oy:8 * oy + 8]
            vol[at, 8 * oy:8 * oy + 8] = both
            pad[1 + 4 * half:5 + 4 * half, 1 + 8 * oy:9 + 8 * oy, :, MID] = both.astype(BF16)

    near_own = 8 - 7 * m
    far_own = 1 + 7 * m
    near_margin_there = 9 * m
    far_margin = 9 * m

    def halo_copies(space, turn):
        copies = []

        def add(src, dst, device):
            at = len(copies)
            copies.append(remote(src, dst, halo_s.at[turn, at], halo_r.at[turn, at], device))

        add(space.at[near_own, 1:17, :, MID], space.at[near_margin_there, 1:17, :, MID], pair)
        for j in range(1, 8):
            there = (wrap(s + sign * j), other)
            if j <= 4:
                add(space.at[far_own, 1:17, :, MID], far[turn].at[j - 1], there)
            add(edges.at[turn], far_edge[turn].at[j - 1], there)
        for j in range(1, 4):
            for step, row, landing in ((j, 16, y_low[turn]), (-j, 1, y_high[turn])):
                at = wrap(s + step)
                add(space.at[1:9, row, :, MID], landing.at[j - 1, 1:9], (at, m))
                add(space.at[near_own, row, :, MID], landing.at[j - 1, near_margin_there], (at, other))
        for step, face, landing in ((1, 1, z_low), (-1, 0, z_high)):
            at = wrap(s + step)
            add(faces.at[turn, face], landing.at[turn, 1:9], (at, m))
            add(faces.at[turn, face, near_own - 1], landing.at[turn, near_margin_there], (at, other))
        return copies

    def stage(space, turn):
        def one(x, _):
            for face, z in ((0, 0), (1, 15)):
                got = vol.at[x].reshape(256, 128)[pl.ds(z, 16, stride=16), :]
                faces[turn, face, x] = got.astype(BF16)
            return 0

        lax.fori_loop(0, 8, one, 0)
        edges[turn, 0] = faces[turn, 0, far_own - 1]
        edges[turn, 1] = space[far_own, 1, :, MID]
        edges[turn, 2] = space[far_own, 16, :, MID]
        edges[turn, 3] = faces[turn, 1, far_own - 1]

    zero = jnp.zeros((), BF16)

    def fill(space, turn):
        def beside(k):
            got = near[0, k]
            return got >= 0, got - s

        there, d = beside(15)
        space[:, 17, :, MID] = jnp.where(there, y_high[turn][jnp.clip(d - 1, 0, 2)], zero)
        there, d = beside(10)
        space[:, 0, :, MID] = jnp.where(there, y_low[turn][jnp.clip(-d - 1, 0, 2)], zero)
        there, d = beside(13)
        margin[1, :, 1:17, :] = jnp.where(there, z_high[turn], zero).astype(F32)
        there, d = beside(12)
        margin[0, :, 1:17, :] = jnp.where(there, z_low[turn], zero).astype(F32)
        for k, landing, to, z in ((16, y_high, 17, 1), (14, y_high, 17, 0), (11, y_low, 0, 1), (9, y_low, 0, 0)):
            there, d = beside(k)
            slot = jnp.clip(jnp.where(d > 0, d, -d) - 1, 0, 2)
            row = 0 if z else 15
            got = jnp.where(there, landing[turn][slot], zero).astype(F32)
            margin[z, :, to:to + 1, :] = got[:, row:row + 1, :]
        for dy in (-1, 0, 1):
            for dz in (-1, 0, 1):
                there, d = beside(17 * m + (dy + 1) * 3 + dz + 1)
                j = sign * d
                slot = jnp.clip(j - 1, 0, 6)
                if dy == 0 and dz == 0:
                    space[far_margin, 1:17, :, MID] = jnp.where(there, far[turn][jnp.clip(j - 1, 0, 3)], zero)
                elif dz == 0:
                    to, edge = (17, 1) if dy == 1 else (0, 2)
                    space[far_margin, to, :, MID] = jnp.where(there, far_edge[turn][slot, edge], zero)
                elif dy == 0:
                    z, edge = (1, 0) if dz == 1 else (0, 3)
                    margin[z, far_margin, 1:17, :] = jnp.where(there, far_edge[turn][slot, edge], zero).astype(F32)
                else:
                    to, edge = (17, 1) if dy == 1 else (0, 2)
                    z, row = (1, 0) if dz == 1 else (0, 15)
                    got = jnp.where(there, far_edge[turn][slot, edge], zero).astype(F32)
                    margin[z, far_margin, to:to + 1, :] = got[row:row + 1, :]

        def one(x, _):
            shift_a[8:296, :] = space[x, :, :, MID].astype(F32).reshape(288, 128)
            for z, start, row in ((0, 7, 0), (1, 9, 15)):
                shift_b[z] = shift_a[start:start + 288, :]
                shift_b.at[z][pl.ds(row, 18, stride=16), :] = margin[z, x]
                lanes = slice(256 * z, 256 * z + 128)
                space[x, :, :, lanes] = shift_b[z].reshape(18, 16, 128).astype(BF16)
            return 0

        lax.fori_loop(0, 10, one, 0)

    def conv_rows(space, weights, chunk):
        total = None
        for ex in range(3):
            for ey in range(3):
                window = space[pl.ds(2 * chunk + ex, 2), ey:ey + 16].reshape(512, 384)
                tap = ex * 9 + ey * 3
                part = dot(window, weights[tap:tap + 3].reshape(384, 128))
                total = part if total is None else total + part
        return total

    stage(pad, 0)
    copies = halo_copies(pad, 0)
    for copy in copies:
        copy.start()
    for copy in copies:
        copy.wait()
    fill(pad, 0)

    def forward(c, _):
        at = pl.ds(2 * c, 2)
        here = mask[at].reshape(512, 128)
        pre = conv_rows(pad, w_conv, c) * here
        sigmoid = 1.0 / (1.0 + jnp.exp(-pre))
        hid[...] = (pre * sigmoid).astype(BF16).astype(F32).reshape(2, 8, 2, 16, 128)
        grad = up[c].reshape(512, 128) * sigmoid * (1.0 + pre * (1.0 - sigmoid)) * here
        grad = grad.astype(BF16)
        grad_wide = grad.astype(F32)
        vol[at] = grad_wide.reshape(2, 16, 16, 128)
        gpad[pl.ds(2 * c + 1, 2), 1:17, :, MID] = grad.reshape(2, 16, 16, 128)
        for x in range(2):
            turned[2 * c + x] = grad_wide[256 * x:256 * x + 256].T.astype(BF16)
        rows = pl.ds(pl.multiple_of(64 * c, 64), 64)
        for tx in range(2):
            for ty in range(2):
                for tz in range(2):
                    t = (tx * 2 + ty) * 2 + tz
                    got = hid[tx, :, ty, pl.ds(tz, 8, stride=2), :].reshape(64, 128)
                    patches[rows, 128 * t:128 * t + 128] = got.astype(BF16)
        return 0

    lax.fori_loop(0, 4, forward, 0)

    stage(gpad, 1)
    grad_copies = halo_copies(gpad, 1)
    for copy in grad_copies:
        copy.start()

    for t in range(8):
        got = lax.dot_general(
            patches[:, 128 * t:128 * t + 128], own_cot, (((0,), (0,)), ((), ())), preferred_element_type=F32
        )
        down_st[0, 128 * t:128 * t + 128, :] = got[:, :128]
        down_st[1, 128 * t:128 * t + 128, :] = got[:, 128:]
    down_swap = remote(down_st.at[other], down_in, pair_s.at[1], pair_r.at[1], pair)
    down_swap.start()
    got = dot(patches[...], w_down[...]).astype(BF16)
    coarse_st[0] = got[:, :128]
    coarse_st[1] = got[:, 128:]
    own_half = pl.ds(pl.multiple_of(m * 256, 256), 256)
    coarse_swap = remote(coarse_st.at[other], coarse.at[own_half], pair_s.at[2], pair_r.at[2], pair)
    coarse_swap.start()
    coarse[own_half, :] = coarse_st[m]
    down_swap.wait()
    down_in[...] = down_in[...] + down_st[m]
    d_bf[...] = down_in[...].reshape(8, 128, 128).astype(BF16)
    d1 = []
    for step in range(1, ZS):
        z, device = line_peer(step)
        d1.append(remote(d_bf.at[z], d_in.at[step - 1], d1_s.at[step - 1], d1_r.at[step - 1], device))
        d1[-1].start()

    conv_swaps = []
    for ex in range(3):
        for ey in range(3):
            total = None
            for half in range(2):
                rows = pad[ex + 4 * half:ex + 4 * half + 4, ey:ey + 16].reshape(1024, 384)
                left = jnp.concatenate([turned[4 * half + x] for x in range(4)], axis=1)
                part = dot(left, rows)
                total = part if total is None else total + part
            for ez in range(3):
                tap = total[:, 128 * ez:128 * ez + 128].T
                at = ex * 9 + ey * 3 + ez
                conv_st[0, 64 * at:64 * at + 64, :] = tap[:64]
                conv_st[1, 64 * at:64 * at + 64, :] = tap[64:]
        rows = slice(576 * ex, 576 * ex + 576)
        conv_swaps.append(
            remote(conv_st.at[other, rows], conv_in.at[rows], pair_s.at[3 + ex], pair_r.at[3 + ex], pair)
        )
        conv_swaps[-1].start()
    for ex in range(3):
        rows = slice(576 * ex, 576 * ex + 576)
        conv_swaps[ex].wait()
        conv_in[rows, :] = conv_in[rows, :] + conv_st[m, rows, :]
    conv_in[1728:, :] = jnp.zeros((320, 128), F32)
    c_bf[...] = conv_in[...].reshape(16, 128, 128).astype(BF16)
    c1 = []
    for at, step in enumerate(plane_steps):
        peer, device = plane_peer(step)
        c1.append(remote(c_bf.at[peer], c_in.at[at], c1_s.at[at], c1_r.at[at], device))
        c1[-1].start()

    for copy in d1:
        copy.wait()
    d_mid[...] = down_in[pl.ds(pl.multiple_of(my_z * 128, 128), 128), :]
    for step in range(ZS - 1):
        d_mid[...] = d_mid[...] + d_in[step].astype(F32)
    d2 = []
    for at, step in enumerate(plane_steps):
        peer, device = plane_peer(step)
        rows = pl.ds(pl.multiple_of(peer * 8, 8), 8)
        d2.append(remote(d_mid.at[rows], d_in2.at[at], d2_s.at[at], d2_r.at[at], device))
        d2[-1].start()

    for copy in grad_copies:
        copy.wait()
    fill(gpad, 1)

    def backward(c, _):
        at = pl.ds(2 * c, 2)
        vol[at] = (conv_rows(gpad, w_back, c) * mask[at].reshape(512, 128)).reshape(2, 16, 16, 128)
        return 0

    lax.fori_loop(0, 2, backward, 0)

    for copy in d2:
        copy.wait()
    total = d_mid[pl.ds(pl.multiple_of(plane * 8, 8), 8), :]
    for at in range(15):
        total = total + d_in2[at]
    d_mix[plane] = total
    d3 = []
    for at, step in enumerate(plane_steps):
        peer, device = plane_peer(step)
        d3.append(remote(d_mix.at[plane], d_mix.at[plane], d3_s.at[at], d3_r.at[at], device))
        d3[-1].start()

    for copy in c1:
        copy.wait()
    own_plane = pl.ds(pl.multiple_of(plane * 128, 128), 128)
    c_mid[...] = conv_in[own_plane, :]
    for at in range(15):
        c_mid[...] = c_mid[...] + c_in[at].astype(F32)
    c2 = []
    for step in range(1, ZS):
        z, device = line_peer(step)
        rows = pl.ds(pl.multiple_of(z * 16, 16), 16)
        c2.append(remote(c_mid.at[rows], c_in2.at[step - 1], c2_s.at[step - 1], c2_r.at[step - 1], device))
        c2[-1].start()

    lax.fori_loop(2, 4, backward, 0)

    for copy in d3:
        copy.wait()
    d_tot[...] = d_mix[...].reshape(128, 128).astype(BF16)
    d_all[my_z] = d_tot[...]
    d4 = []
    for step in range(1, ZS):
        z, device = line_peer(step)
        d4.append(remote(d_tot, d_all.at[my_z], d4_s.at[step - 1], d4_r.at[step - 1], device))
        d4[-1].start()
    for copy in c2:
        copy.wait()
    own_line = pl.ds(pl.multiple_of(my_z * 16, 16), 16)
    total = c_mid[own_line, :]
    for step in range(ZS - 1):
        total = total + c_in2[step]
    c_tot[...] = total.astype(BF16)
    c_all[plane, own_line, :] = c_tot[...]
    c3 = []
    for step in range(1, ZS):
        z, device = line_peer(step)
        c3.append(remote(c_tot, c_all.at[plane, own_line], c3_s.at[step - 1], c3_r.at[step - 1], device))
        c3[-1].start()

    for oy in range(2):
        for oz in range(2):
            got = vol[:, 8 * oy:8 * oy + 8, 8 * oz:8 * oz + 8, :].reshape(512, 128)
            for part in range(2):
                columns = slice(256 * part, 256 * part + 256)
                out_bricks[oy + 2 * oz, :, columns] = got[columns].T.astype(BF16)
    feat_swap = remote(out_bricks.at[:, other_rows, :], g_feat.at[:, m], pair_s.at[6], pair_r.at[6], pair)
    feat_swap.start()
    g_feat[:, m] = out_bricks[:, own_rows, :]

    for copy in c3:
        copy.wait()
    c4 = []
    for at, step in enumerate(plane_steps):
        peer, device = plane_peer(step)
        c4.append(remote(c_all.at[plane], c_all.at[plane], c4_s.at[at], c4_r.at[at], device))
        c4[-1].start()
    for copy in d4:
        copy.wait()
    g_down[...] = d_all[...].reshape(1024, 128).astype(F32) * (1.0 / BLOCKS)
    coarse_swap.wait()
    feat_swap.wait()
    for copy in c4:
        copy.wait()
    g_conv[...] = c_all[...].reshape(2048, 128)[:1728].astype(F32) * (1.0 / BLOCKS)


def local(features, heights, neighbours, w_conv, w_down, cotangent):
    vmem = pl.BlockSpec(memory_space=pltpu.VMEM)
    smem = pl.BlockSpec(memory_space=pltpu.SMEM)
    dma = pltpu.SemaphoreType.DMA
    V = pltpu.VMEM
    scratch = [
        V((10, 18, 16, 384), BF16),
        V((10, 18, 16, 384), BF16),
        V((8, 16, 16, 128), F32),
        V((4, 2, 8, 2, 16, 128), F32),
        V((8, 16, 16, 128), F32),
        V((4, 128, 512), BF16),
        V((2, 8, 2, 16, 128), F32),
        V((256, 1024), BF16),
        V((8, 128, 256), BF16),
        V((27, 128, 128), BF16),
        V((4, 128, 512), BF16),
        V((304, 128), F32),
        V((2, 288, 128), F32),
        V((2, 10, 18, 128), F32),
        V((2, 2, 8, 16, 128), BF16),
        V((2, 4, 16, 128), BF16),
        V((3, 10, 16, 128), BF16), V((3, 10, 16, 128), BF16),
        V((3, 10, 16, 128), BF16), V((3, 10, 16, 128), BF16),
        V((2, 10, 16, 128), BF16),
        V((2, 10, 16, 128), BF16),
        V((4, 16, 16, 128), BF16), V((4, 16, 16, 128), BF16),
        V((7, 4, 16, 128), BF16), V((7, 4, 16, 128), BF16),
        V((2, 256, 128), BF16),
        V((2, 1024, 128), F32),
        V((1024, 128), F32),
        V((2, 1728, 128), F32),
        V((2048, 128), F32),
        V((16, 128, 128), BF16),
        V((15, 128, 128), BF16),
        V((128, 128), F32),
        V((7, 16, 128), F32),
        V((16, 128), BF16),
        V((16, 128, 128), BF16),
        V((8, 128, 128), BF16),
        V((7, 128, 128), BF16),
        V((128, 128), F32),
        V((15, 8, 128), F32),
        V((128, 128), BF16),
        V((16, 8, 128), F32),
        V((8, 128, 128), BF16),
        dma((2, 28)), dma((2, 28)), dma((7,)), dma((7,)),
        dma((15,)), dma((15,)), dma((7,)), dma((7,)), dma((7,)), dma((7,)), dma((15,)), dma((15,)),
        dma((7,)), dma((7,)), dma((15,)), dma((15,)), dma((15,)), dma((15,)), dma((7,)), dma((7,)),
    ]
    coarse, g_conv, g_down, g_feat = pl.pallas_call(
        kernel,
        out_shape=(
            jax.ShapeDtypeStruct((512, 128), BF16),
            jax.ShapeDtypeStruct((1728, 128), F32),
            jax.ShapeDtypeStruct((1024, 128), F32),
            jax.ShapeDtypeStruct((4, 2, 64, 512), BF16),
        ),
        in_specs=[smem, smem, vmem, vmem, vmem, vmem],
        out_specs=(vmem, vmem, vmem, vmem),
        scratch_shapes=scratch,
        compiler_params=pltpu.CompilerParams(
            collective_id=0, has_side_effects=True, vmem_limit_bytes=56 * 2**20
        ),
        cost_estimate=pl.CostEstimate(
            flops=6_000_000_000, bytes_accessed=6_000_000, transcendentals=262144
        ),
    )(
        heights,
        neighbours,
        features.transpose(0, 2, 1).reshape(4, 2, 64, 512),
        w_conv,
        w_down.reshape(1024, 256),
        cotangent[0],
    )
    return (
        coarse[None],
        g_conv.reshape(27, 64, 128),
        g_down.reshape(8, 128, 128),
        g_feat.reshape(8, 64, 512).transpose(0, 2, 1),
    )


def solution(mesh):
    placed = (
        P("space", None, "chan"),
        P("space", None),
        P("space", None),
        P(),
        P(),
        P("space", None, None),
    )
    return jax.shard_map(
        local,
        mesh=mesh,
        in_specs=placed,
        out_specs=(
            P("space", None, "chan"),
            P(None, "chan", None),
            P(None, None, "chan"),
            P("space", None, "chan"),
        ),
        check_vma=False,
    )
```

```python
import jax
import jax.numpy as jnp
from jax import lax
from jax.experimental import pallas as pl
from jax.experimental.pallas import tpu as pltpu
from jax.sharding import PartitionSpec as P

MESH = pl.DeviceIdType.MESH
F32 = jnp.float32
BF16 = jnp.bfloat16
MID = slice(128, 256)
XS, ZS, YS = 4, 8, 4
BLOCKS = XS * ZS * YS


def dot(a, b):
    return jnp.dot(a, b, preferred_element_type=F32)


def dot_t(a, b):
    return lax.dot_general(a, b, (((1,), (1,)), ((), ())), preferred_element_type=F32)


def kernel(
    heights, near, feat, w_conv_far, w_down_far, cot_far,
    coarse, c_out, d_out, g_feat,
    w_conv, w_down, cot,
    pad, gpad, mask, up, vol, cat, hid, patches, turned, w_back, out_bricks,
    shift_a, shift_b, margin,
    faces, edges, lines, y_low_0, y_low_1, y_high_0, y_high_1, z_low, z_high, far_0, far_1, far_edge_0, far_edge_1,
    line_in,
    coarse_st, down_st, down_in, conv_st, conv_in,
    c_bf, c_in, c_line, c_tot, d_bf, d_in, d_plane, d_tot,
    load, halo_s, halo_r, pair_s, pair_r,
    c1_s, c1_r, c2_s, c2_r, c3_s, c3_r, d1_s, d1_r, d2_s, d2_r, d3_s, d3_r,
):
    y_low, y_high = (y_low_0, y_low_1), (y_high_0, y_high_1)
    far, far_edge = (far_0, far_1), (far_edge_0, far_edge_1)
    s = lax.axis_index("space")
    m = lax.axis_index("chan")
    other = 1 - m
    sign = 2 * m - 1
    my_y = s % YS
    my_z = s // YS % ZS
    my_x = s // (YS * ZS)
    plane = my_x * YS + my_y
    wrap = lambda index: (index + 2 * BLOCKS) % BLOCKS
    plane_steps = [(a, b) for a in range(XS) for b in range(YS) if (a, b) != (0, 0)]

    def plane_peer(step):
        x, y = (my_x + step[0]) % XS, (my_y + step[1]) % YS
        return x * YS + y, ((x * ZS + my_z) * YS + y, m)

    def line_peer(step):
        z = (my_z + step) % ZS
        return z, ((my_x * ZS + z) * YS + my_y, m)

    def remote(src, dst, send, recv, device):
        return pltpu.make_async_remote_copy(
            src_ref=src, dst_ref=dst, send_sem=send, recv_sem=recv, device_id=device, device_id_type=MESH
        )

    barrier = pltpu.get_barrier_semaphore()
    greeted = [(s, other)]
    for d in (1, 2, 3):
        for e in (d, -d):
            greeted += [(wrap(s + e), m), (wrap(s + e), other)]
    greeted += [(wrap(s + sign * j), other) for j in (4, 5, 6, 7)]
    greeted += [plane_peer(step)[1] for step in plane_steps]
    greeted += [line_peer(step)[1] for step in range(1, ZS)]
    for device in greeted:
        pl.semaphore_signal(barrier, inc=1, device_id=device, device_id_type=MESH)

    pair = (s, other)
    own_rows = pl.ds(pl.multiple_of(m * 64, 64), 64)
    other_rows = pl.ds(pl.multiple_of(other * 64, 64), 64)
    own_half = pl.ds(pl.multiple_of(m * 256, 256), 256)
    feat_own = pltpu.make_async_copy(feat.at[:, m], cat.at[:, own_rows, :], load.at[0])
    loads = [
        pltpu.make_async_copy(w_down_far, w_down, load.at[1]),
        pltpu.make_async_copy(cot_far.at[own_half], cot, load.at[2]),
        pltpu.make_async_copy(w_conv_far, w_conv, load.at[3]),
    ]
    feat_own.start()
    for copy in loads:
        copy.start()

    pl.semaphore_wait(barrier, len(greeted))

    swap = remote(feat.at[:, other], cat.at[:, own_rows, :], pair_s.at[0], pair_r.at[0], pair)
    swap.start()
    levels = lax.broadcasted_iota(jnp.int32, (8, 128), 0)

    def mask_plane(x, _):
        for y in range(16):
            for z in range(2):
                height = heights[m + 2 * (y // 8) + 4 * z, x * 8 + y % 8]
                mask[x, y, 8 * z:8 * z + 8, :] = jnp.where(levels < height, 1.0, 0.0)
        return 0

    lax.fori_loop(0, 8, mask_plane, 0)
    feat_own.wait()
    swap.wait()

    for oy in range(2):
        for half in range(2):
            columns = slice(256 * half, 256 * half + 256)
            low = cat[oy, :, columns].astype(F32).T.reshape(4, 8, 8, 128)
            high = cat[oy + 2, :, columns].astype(F32).T.reshape(4, 8, 8, 128)
            both = jnp.concatenate([low, high], axis=2)
            at = slice(4 * half, 4 * half + 4)
            both = both * mask[at, 8 * oy:8 * oy + 8]
            vol[at, 8 * oy:8 * oy + 8] = both
            pad[1 + 4 * half:5 + 4 * half, 1 + 8 * oy:9 + 8 * oy, :, MID] = both.astype(BF16)

    near_own = 8 - 7 * m
    far_own = 1 + 7 * m
    near_margin_there = 9 * m
    near_margin = 9 - 9 * m
    far_margin = 9 * m

    def halo_copies(space, turn):
        copies = []

        def add(src, dst, device):
            at = len(copies)
            copies.append(remote(src, dst, halo_s.at[turn, at], halo_r.at[turn, at], device))

        for j in (2, 1, 3, 4):
            there = (wrap(s + sign * j), other)
            add(space.at[far_own, 1:17, :, MID], far[turn].at[j - 1], there)
        for j in (2, 1):
            for step, row, landing in ((j, 16, y_low[turn]), (-j, 1, y_high[turn])):
                at = wrap(s + step)
                add(space.at[1:9, row, :, MID], landing.at[j - 1, 1:9], (at, m))
                add(space.at[near_own, row, :, MID], landing.at[j - 1, near_margin_there], (at, other))
        for step, face, landing in ((1, 1, z_low), (-1, 0, z_high)):
            at = wrap(s + step)
            add(faces.at[turn, face], landing.at[turn, 1:9], (at, m))
            add(faces.at[turn, face, near_own - 1], landing.at[turn, near_margin_there], (at, other))
        for j in range(1, 8):
            there = (wrap(s + sign * j), other)
            which = slice(1, 3) if j <= 4 else pl.ds(2 * m, 2)
            add(edges.at[turn, which], far_edge[turn].at[j - 1, which], there)
        for step, line, side in ((3, 1, 0), (-3, 0, 1)):
            at = wrap(s + step)
            add(lines.at[turn, line], line_in.at[turn, side, 0], (at, m))
            add(lines.at[turn, line], line_in.at[turn, side, 1], (at, other))
        add(space.at[near_own, 1:17, :, MID], space.at[near_margin_there, 1:17, :, MID], pair)
        return copies

    def stage(space, turn):
        def one(x, _):
            for face, z in ((0, 0), (1, 15)):
                got = vol.at[x].reshape(256, 128)[pl.ds(z, 16, stride=16), :]
                faces[turn, face, x] = got.astype(BF16)
            return 0

        lax.fori_loop(0, 8, one, 0)
        for line, start in ((0, 0), (1, 255)):
            got = vol.reshape(2048, 128)[pl.ds(start, 8, stride=256), :]
            lines[turn, line] = jnp.concatenate([got, got], axis=0).astype(BF16)
        edges[turn, 0] = space[far_own, 1, :, MID]
        edges[turn, 1] = faces[turn, 0, far_own - 1]
        edges[turn, 2] = faces[turn, 1, far_own - 1]
        edges[turn, 3] = space[far_own, 16, :, MID]

    zero = jnp.zeros((), BF16)

    def fill(space, turn):
        def beside(k):
            got = near[0, k]
            return got >= 0, got - s

        there, d = beside(15)
        space[:, 17, :, MID] = jnp.where(there, y_high[turn][jnp.clip(d - 1, 0, 1)], zero)
        there, d = beside(10)
        space[:, 0, :, MID] = jnp.where(there, y_low[turn][jnp.clip(-d - 1, 0, 1)], zero)
        there, d = beside(13)
        margin[1, :, 1:17, :] = jnp.where(there, z_high[turn], zero).astype(F32)
        there, d = beside(12)
        margin[0, :, 1:17, :] = jnp.where(there, z_low[turn], zero).astype(F32)
        for k, landing, to, z in ((16, y_high, 17, 1), (14, y_high, 17, 0), (11, y_low, 0, 1), (9, y_low, 0, 0)):
            there, d = beside(k)
            j = jnp.where(d > 0, d, -d)
            row = 0 if z else 15
            got = jnp.where(there, landing[turn][jnp.clip(j - 1, 0, 1)], zero).astype(F32)
            got = got[:, row:row + 1, :]
            margin[z, :, to:to + 1, :] = got
            if k in (16, 9):
                side = 1 if k == 16 else 0
                third = there & (j == 3)
                line = line_in[turn, side, 0].astype(F32)[:8].reshape(8, 1, 128)
                margin[z, 1:9, to:to + 1, :] = jnp.where(third, line, got[1:9])
                beyond = line_in[turn, side, 1].astype(F32)
                beyond = jnp.where(m == 0, beyond[0:1], beyond[7:8])
                margin[z, near_margin, to:to + 1, :] = jnp.where(
                    third, beyond, jnp.where(m == 0, got[9], got[0])
                )
        for dy in (-1, 0, 1):
            for dz in (-1, 0, 1):
                there, d = beside(17 * m + (dy + 1) * 3 + dz + 1)
                j = sign * d
                slot = jnp.clip(j - 1, 0, 6)
                slot_4 = jnp.clip(j - 1, 0, 3)
                if dy == 0 and dz == 0:
                    space[far_margin, 1:17, :, MID] = jnp.where(there, far[turn][slot_4], zero)
                elif dy == 0:
                    z, edge = (1, 1) if dz == 1 else (0, 2)
                    margin[z, far_margin, 1:17, :] = jnp.where(there, far_edge[turn][slot, edge], zero).astype(F32)
                else:
                    to, edge, at = (17, 0, 0) if dy == 1 else (0, 3, 15)
                    got = jnp.where(j <= 4, far[turn][slot_4, at], far_edge[turn][slot, edge])
                    got = jnp.where(there, got, zero)
                    if dz == 0:
                        space[far_margin, to, :, MID] = got
                    else:
                        z, row = (1, 0) if dz == 1 else (0, 15)
                        margin[z, far_margin, to:to + 1, :] = got.astype(F32)[row:row + 1, :]

        def one(x, _):
            shift_a[8:296, :] = space[x, :, :, MID].astype(F32).reshape(288, 128)
            for z, start, row in ((0, 7, 0), (1, 9, 15)):
                shift_b[z] = shift_a[start:start + 288, :]
                shift_b.at[z][pl.ds(row, 18, stride=16), :] = margin[z, x]
                lanes = slice(256 * z, 256 * z + 128)
                space[x, :, :, lanes] = shift_b[z].reshape(18, 16, 128).astype(BF16)
            return 0

        lax.fori_loop(0, 10, one, 0)

    def conv_rows(space, weights, chunk):
        total = None
        for ex in range(3):
            for ey in range(3):
                window = space[pl.ds(2 * chunk + ex, 2), ey:ey + 16].reshape(512, 384)
                tap = ex * 9 + ey * 3
                part = dot(window, weights[tap:tap + 3].reshape(384, 128))
                total = part if total is None else total + part
        return total

    stage(pad, 0)
    copies = halo_copies(pad, 0)
    for copy in copies:
        copy.start()

    for copy in loads:
        copy.wait()

    def upstream(t, _):
        rows = w_down[pl.ds(pl.multiple_of(t * 256, 256), 256), :]
        got = dot_t(cot[...], rows)
        for z in range(2):
            part = got[:, 128 * z:128 * z + 128].reshape(4, 8, 8, 128)
            for x in range(4):
                up[x, t // 2, :, t % 2, pl.ds(z, 8, stride=2), :] = part[x]
        return 0

    lax.fori_loop(0, 4, upstream, 0)

    def turn_back(tap, _):
        w_back[tap] = w_conv[26 - tap].astype(F32).T.astype(BF16)
        return 0

    lax.fori_loop(0, 27, turn_back, 0)

    for copy in copies:
        copy.wait()
    fill(pad, 0)

    def forward(c, _):
        at = pl.ds(2 * c, 2)
        here = mask[at].reshape(512, 128)
        pre = conv_rows(pad, w_conv, c) * here
        sigmoid = 1.0 / (1.0 + jnp.exp(-pre))
        hid[...] = (pre * sigmoid).astype(BF16).astype(F32).reshape(2, 8, 2, 16, 128)
        grad = up[c].reshape(512, 128) * sigmoid * (1.0 + pre * (1.0 - sigmoid)) * here
        grad = grad.astype(BF16)
        grad_wide = grad.astype(F32)
        vol[at] = grad_wide.reshape(2, 16, 16, 128)
        gpad[pl.ds(2 * c + 1, 2), 1:17, :, MID] = grad.reshape(2, 16, 16, 128)
        for x in range(2):
            turned[2 * c + x] = grad_wide[256 * x:256 * x + 256].T.astype(BF16)
        rows = pl.ds(pl.multiple_of(64 * c, 64), 64)
        for tx in range(2):
            for ty in range(2):
                for tz in range(2):
                    t = (tx * 2 + ty) * 2 + tz
                    got = hid[tx, :, ty, pl.ds(tz, 8, stride=2), :].reshape(64, 128)
                    patches[rows, 128 * t:128 * t + 128] = got.astype(BF16)
        return 0

    lax.fori_loop(0, 4, forward, 0)

    for t in range(8):
        got = lax.dot_general(
            patches[:, 128 * t:128 * t + 128], cot[...], (((0,), (0,)), ((), ())), preferred_element_type=F32
        )
        down_st[0, 128 * t:128 * t + 128, :] = got[:, :128]
        down_st[1, 128 * t:128 * t + 128, :] = got[:, 128:]
    down_swap = remote(down_st.at[other], down_in, pair_s.at[1], pair_r.at[1], pair)
    down_swap.start()

    conv_swaps = []
    d1 = []
    for ex in range(3):
        for ey in range(3):
            total = None
            for half in range(2):
                rows = pad[ex + 4 * half:ex + 4 * half + 4, ey:ey + 16].reshape(1024, 384)
                left = jnp.concatenate([turned[4 * half + x] for x in range(4)], axis=1)
                part = dot(left, rows)
                total = part if total is None else total + part
            for ez in range(3):
                tap = total[:, 128 * ez:128 * ez + 128].T
                at = ex * 9 + ey * 3 + ez
                conv_st[0, 64 * at:64 * at + 64, :] = tap[:64]
                conv_st[1, 64 * at:64 * at + 64, :] = tap[64:]
        rows = slice(576 * ex, 576 * ex + 576)
        conv_swaps.append(
            remote(conv_st.at[other, rows], conv_in.at[rows], pair_s.at[3 + ex], pair_r.at[3 + ex], pair)
        )
        conv_swaps[-1].start()
        if ex == 1:
            down_swap.wait()
            down_in[...] = down_in[...] + down_st[m]
            d_bf[...] = down_in[...].reshape(8, 128, 128).astype(BF16)
            for step in range(1, ZS):
                z, device = line_peer(step)
                d1.append(remote(d_bf.at[z], d_in.at[step - 1], d1_s.at[step - 1], d1_r.at[step - 1], device))
                d1[-1].start()
    conv_in[1728:, :] = jnp.zeros((64, 128), F32)
    for ex in range(3):
        rows = slice(576 * ex, 576 * ex + 576)
        conv_swaps[ex].wait()
        conv_in[rows, :] = conv_in[rows, :] + conv_st[m, rows, :]
    c_bf[...] = conv_in[...].reshape(16, 112, 128).astype(BF16)
    c1 = []
    for at, step in enumerate(plane_steps):
        peer, device = plane_peer(step)
        c1.append(remote(c_bf.at[peer], c_in.at[at], c1_s.at[at], c1_r.at[at], device))
        c1[-1].start()

    stage(gpad, 1)
    grad_copies = halo_copies(gpad, 1)
    for copy in grad_copies:
        copy.start()
    got = dot(patches[...], w_down[...]).astype(BF16)
    coarse_st[0] = got[:, :128]
    coarse_st[1] = got[:, 128:]
    coarse_swap = remote(coarse_st.at[other], coarse.at[own_half], pair_s.at[2], pair_r.at[2], pair)
    coarse_swap.start()
    coarse_own = pltpu.make_async_copy(coarse_st.at[m], coarse.at[own_half], load.at[4])
    coarse_own.start()

    for copy in d1:
        copy.wait()
    total = down_in[pl.ds(pl.multiple_of(my_z * 128, 128), 128), :]
    for step in range(ZS - 1):
        total = total + d_in[step].astype(F32)
    d_plane[plane] = total.astype(BF16)
    d2 = []
    for at, step in enumerate(plane_steps):
        peer, device = plane_peer(step)
        d2.append(remote(d_plane.at[plane], d_plane.at[plane], d2_s.at[at], d2_r.at[at], device))
        d2[-1].start()

    for copy in c1:
        copy.wait()
    total = conv_in[pl.ds(pl.multiple_of(plane * 112, 112), 112), :]
    for at in range(15):
        total = total + c_in[at].astype(F32)
    c_line[my_z] = total.astype(BF16)
    c2 = []
    for step in range(1, ZS):
        z, device = line_peer(step)
        c2.append(remote(c_line.at[my_z], c_line.at[my_z], c2_s.at[step - 1], c2_r.at[step - 1], device))
        c2[-1].start()

    for copy in grad_copies:
        copy.wait()
    fill(gpad, 1)

    def backward(c, _):
        at = pl.ds(2 * c, 2)
        vol[at] = (conv_rows(gpad, w_back, c) * mask[at].reshape(512, 128)).reshape(2, 16, 16, 128)
        return 0

    lax.fori_loop(0, 1, backward, 0)

    for copy in c2:
        copy.wait()
    total = c_line[0].astype(F32)
    for z in range(1, ZS):
        total = total + c_line[z].astype(F32)
    c_tot[...] = total.astype(BF16)
    c3 = []
    for at, step in enumerate(plane_steps):
        peer, device = plane_peer(step)
        c3.append(remote(c_tot, c_out.at[plane], c3_s.at[at], c3_r.at[at], device))
        c3[-1].start()
    c_own = pltpu.make_async_copy(c_tot, c_out.at[plane], load.at[5])
    c_own.start()

    for copy in d2:
        copy.wait()
    total = d_plane[0].astype(F32)
    for at in range(1, 16):
        total = total + d_plane[at].astype(F32)
    d_tot[...] = total.astype(BF16)
    d3 = []
    for step in range(1, ZS):
        z, device = line_peer(step)
        d3.append(remote(d_tot, d_out.at[my_z], d3_s.at[step - 1], d3_r.at[step - 1], device))
        d3[-1].start()
    d_own = pltpu.make_async_copy(d_tot, d_out.at[my_z], load.at[6])
    d_own.start()

    lax.fori_loop(1, 4, backward, 0)

    for oy in range(2):
        for oz in range(2):
            got = vol[:, 8 * oy:8 * oy + 8, 8 * oz:8 * oz + 8, :].reshape(512, 128)
            for part in range(2):
                columns = slice(256 * part, 256 * part + 256)
                out_bricks[oy + 2 * oz, :, columns] = got[columns].T.astype(BF16)
    feat_swap = remote(out_bricks.at[:, other_rows, :], g_feat.at[:, m], pair_s.at[6], pair_r.at[6], pair)
    feat_swap.start()
    feat_out = pltpu.make_async_copy(out_bricks.at[:, own_rows, :], g_feat.at[:, m], load.at[7])
    feat_out.start()

    for copy in c3 + d3 + [coarse_swap, feat_swap, coarse_own, c_own, d_own, feat_out]:
        copy.wait()


def hand_on(c_in, d_in, coarse_in, feat_in, g_conv, g_down, coarse, g_feat, c, d, c_wide, d_wide, co, f, sems):
    held = (c, d, co, f)
    moves = [pltpu.make_async_copy(a, b, sems.at[i]) for i, (a, b) in enumerate(zip((c_in, d_in, coarse_in, feat_in), held))]
    for move in moves:
        move.start()

    def out(at, src, dst):
        move = pltpu.make_async_copy(src, dst, sems.at[at])
        move.start()
        return move

    outs = []
    moves[0].wait()
    for part in range(2):
        rows = slice(864 * part, 864 * part + 864)
        c_wide[rows, :] = c[...].reshape(1792, 128)[rows].astype(F32) * (1.0 / BLOCKS)
        outs.append(out(4 + part, c_wide.at[rows], g_conv.at[rows]))
    moves[1].wait()
    d_wide[...] = d[...].reshape(1024, 128).astype(F32) * (1.0 / BLOCKS)
    outs.append(out(6, d_wide, g_down))
    moves[2].wait()
    outs.append(out(7, co, coarse))
    moves[3].wait()
    outs.append(out(8, f, g_feat))
    for move in outs:
        move.wait()


def local(features, heights, neighbours, w_conv, w_down, cotangent):
    anywhere = pl.BlockSpec(memory_space=pl.ANY)
    smem = pl.BlockSpec(memory_space=pltpu.SMEM)
    dma = pltpu.SemaphoreType.DMA
    V = pltpu.VMEM
    scratch = [
        V((27, 128, 128), BF16), V((1024, 256), BF16), V((256, 256), BF16),
        V((10, 18, 16, 384), BF16),
        V((10, 18, 16, 384), BF16),
        V((8, 16, 16, 128), F32),
        V((4, 2, 8, 2, 16, 128), F32),
        V((8, 16, 16, 128), F32),
        V((4, 128, 512), BF16),
        V((2, 8, 2, 16, 128), F32),
        V((256, 1024), BF16),
        V((8, 128, 256), BF16),
        V((27, 128, 128), BF16),
        V((4, 128, 512), BF16),
        V((304, 128), F32),
        V((2, 288, 128), F32),
        V((2, 10, 18, 128), F32),
        V((2, 2, 8, 16, 128), BF16),
        V((2, 4, 16, 128), BF16),
        V((2, 2, 16, 128), BF16),
        V((2, 10, 16, 128), BF16), V((2, 10, 16, 128), BF16),
        V((2, 10, 16, 128), BF16), V((2, 10, 16, 128), BF16),
        V((2, 10, 16, 128), BF16),
        V((2, 10, 16, 128), BF16),
        V((4, 16, 16, 128), BF16), V((4, 16, 16, 128), BF16),
        V((7, 4, 16, 128), BF16), V((7, 4, 16, 128), BF16),
        V((2, 2, 2, 16, 128), BF16),
        V((2, 256, 128), BF16),
        V((2, 1024, 128), F32),
        V((1024, 128), F32),
        V((2, 1728, 128), F32),
        V((1792, 128), F32),
        V((16, 112, 128), BF16),
        V((15, 112, 128), BF16),
        V((8, 112, 128), BF16),
        V((112, 128), BF16),
        V((8, 128, 128), BF16),
        V((7, 128, 128), BF16),
        V((16, 128, 128), BF16),
        V((128, 128), BF16),
        dma((8,)), dma((2, 28)), dma((2, 28)), dma((7,)), dma((7,)),
        dma((15,)), dma((15,)), dma((7,)), dma((7,)), dma((15,)), dma((15,)),
        dma((7,)), dma((7,)), dma((15,)), dma((15,)), dma((7,)), dma((7,)),
    ]
    made = pl.pallas_call(
        kernel,
        out_shape=(
            jax.ShapeDtypeStruct((512, 128), BF16),
            jax.ShapeDtypeStruct((16, 112, 128), BF16),
            jax.ShapeDtypeStruct((8, 128, 128), BF16),
            jax.ShapeDtypeStruct((4, 2, 64, 512), BF16),
        ),
        in_specs=[smem, smem, anywhere, anywhere, anywhere, anywhere],
        out_specs=(anywhere,) * 4,
        scratch_shapes=scratch,
        compiler_params=pltpu.CompilerParams(
            collective_id=0, has_side_effects=True, vmem_limit_bytes=58 * 2**20
        ),
        cost_estimate=pl.CostEstimate(
            flops=6_000_000_000, bytes_accessed=6_000_000, transcendentals=262144
        ),
    )(
        heights,
        neighbours,
        features.transpose(0, 2, 1).reshape(4, 2, 64, 512),
        w_conv,
        w_down.reshape(1024, 256),
        cotangent[0],
    )
    coarse, g_conv, g_down, g_feat = made
    g_conv, g_down, coarse, g_feat = pl.pallas_call(
        hand_on,
        out_shape=(
            jax.ShapeDtypeStruct((1728, 128), F32),
            jax.ShapeDtypeStruct((1024, 128), F32),
            jax.ShapeDtypeStruct((512, 128), BF16),
            jax.ShapeDtypeStruct((4, 2, 64, 512), BF16),
        ),
        in_specs=[anywhere] * 4,
        out_specs=(anywhere,) * 4,
        scratch_shapes=[
            V((16, 112, 128), BF16), V((8, 128, 128), BF16), V((1728, 128), F32), V((1024, 128), F32),
            V((512, 128), BF16), V((4, 2, 64, 512), BF16), dma((9,)),
        ],
        compiler_params=pltpu.CompilerParams(vmem_limit_bytes=58 * 2**20),
    )(g_conv, g_down, coarse, g_feat)
    return (
        coarse[None],
        g_conv.reshape(27, 64, 128),
        g_down.reshape(8, 128, 128),
        g_feat.reshape(8, 64, 512).transpose(0, 2, 1),
    )


def solution(mesh):
    placed = (
        P("space", None, "chan"),
        P("space", None),
        P("space", None),
        P(),
        P(),
        P("space", None, None),
    )
    return jax.shard_map(
        local,
        mesh=mesh,
        in_specs=placed,
        out_specs=(
            P("space", None, "chan"),
            P(None, "chan", None),
            P(None, None, "chan"),
            P("space", None, "chan"),
        ),
        check_vma=False,
    )
```

```python
import functools

import jax
import jax.numpy as jnp
from jax import lax
from jax.experimental import pallas as pl
from jax.experimental.pallas import tpu as pltpu
from jax.sharding import PartitionSpec as P

MESH = pl.DeviceIdType.MESH
F32 = jnp.float32
BF16 = jnp.bfloat16
MID = slice(128, 256)
XS, ZS, YS = 4, 8, 4
BLOCKS = XS * ZS * YS


def dot(a, b):
    return jnp.dot(a, b, preferred_element_type=F32)


def dot_t(a, b):
    return lax.dot_general(a, b, (((1,), (1,)), ((), ())), preferred_element_type=F32)


def kernel(
    heights_far, near_far, feat, w_conv_far, w_down_far, cot_far,
    coarse, c_out, d_out, g_feat,
    heights, near, w_conv, w_down, cot,
    pad, gpad, mask, up, vol, cat, hid, patches, turned, w_back, out_bricks,
    shift_a, shift_b, margin,
    faces, edges, lines, y_low_0, y_low_1, y_high_0, y_high_1, z_low, z_high, far_0, far_1, far_edge_0, far_edge_1,
    line_in,
    coarse_st, down_st, down_in, conv_st, conv_in,
    c_bf, c_in, c_line, c_tot, d_bf, d_in, d_mid, d_in2, d_mix, d_tot,
    load, halo_s, halo_r, pair_s, pair_r,
    c1_s, c1_r, c2_s, c2_r, c3_s, c3_r, d1_s, d1_r, d2_s, d2_r, d3_s, d3_r, d4_s, d4_r,
):
    y_low, y_high = (y_low_0, y_low_1), (y_high_0, y_high_1)
    far, far_edge = (far_0, far_1), (far_edge_0, far_edge_1)
    s = lax.axis_index("space")
    m = lax.axis_index("chan")
    other = 1 - m
    sign = 2 * m - 1
    my_y = s % YS
    my_z = s // YS % ZS
    my_x = s // (YS * ZS)
    plane = my_x * YS + my_y
    wrap = lambda index: (index + 2 * BLOCKS) % BLOCKS
    plane_steps = [(a, b) for a in range(XS) for b in range(YS) if (a, b) != (0, 0)]

    def plane_peer(step):
        x, y = (my_x + step[0]) % XS, (my_y + step[1]) % YS
        return x * YS + y, ((x * ZS + my_z) * YS + y, m)

    def line_peer(step):
        z = (my_z + step) % ZS
        return z, ((my_x * ZS + z) * YS + my_y, m)

    def remote(src, dst, send, recv, device):
        return pltpu.make_async_remote_copy(
            src_ref=src, dst_ref=dst, send_sem=send, recv_sem=recv, device_id=device, device_id_type=MESH
        )

    barrier = pltpu.get_barrier_semaphore()
    greeted = [(s, other)]
    for d in (1, 2, 3):
        for e in (d, -d):
            greeted += [(wrap(s + e), m), (wrap(s + e), other)]
    greeted += [(wrap(s + sign * j), other) for j in (4, 5, 6, 7)]
    greeted += [plane_peer(step)[1] for step in plane_steps]
    greeted += [line_peer(step)[1] for step in range(1, ZS)]
    for device in greeted:
        pl.semaphore_signal(barrier, inc=1, device_id=device, device_id_type=MESH)

    pair = (s, other)
    own_rows = pl.ds(pl.multiple_of(m * 64, 64), 64)
    other_rows = pl.ds(pl.multiple_of(other * 64, 64), 64)
    own_half = pl.ds(pl.multiple_of(m * 256, 256), 256)
    feat_own = pltpu.make_async_copy(feat.at[:, m], cat.at[:, own_rows, :], load.at[0])
    loads = [
        pltpu.make_async_copy(w_down_far, w_down, load.at[1]),
        pltpu.make_async_copy(cot_far.at[own_half], cot, load.at[2]),
        pltpu.make_async_copy(w_conv_far, w_conv, load.at[3]),
    ]
    scalars = [
        pltpu.make_async_copy(heights_far, heights, load.at[8]),
        pltpu.make_async_copy(near_far, near, load.at[9]),
    ]
    for copy in scalars + [feat_own] + loads:
        copy.start()

    pl.semaphore_wait(barrier, len(greeted))

    swap = remote(feat.at[:, other], cat.at[:, own_rows, :], pair_s.at[0], pair_r.at[0], pair)
    swap.start()
    for copy in scalars:
        copy.wait()
    levels = lax.broadcasted_iota(jnp.int32, (8, 128), 0)

    def mask_plane(x, _):
        for y in range(16):
            for z in range(2):
                height = heights[m + 2 * (y // 8) + 4 * z, x * 8 + y % 8]
                mask[x, y, 8 * z:8 * z + 8, :] = jnp.where(levels < height, 1.0, 0.0)
        return 0

    lax.fori_loop(0, 8, mask_plane, 0)
    feat_own.wait()
    swap.wait()

    for oy in range(2):
        for half in range(2):
            columns = slice(256 * half, 256 * half + 256)
            low = cat[oy, :, columns].astype(F32).T.reshape(4, 8, 8, 128)
            high = cat[oy + 2, :, columns].astype(F32).T.reshape(4, 8, 8, 128)
            both = jnp.concatenate([low, high], axis=2)
            at = slice(4 * half, 4 * half + 4)
            both = both * mask[at, 8 * oy:8 * oy + 8]
            vol[at, 8 * oy:8 * oy + 8] = both
            pad[1 + 4 * half:5 + 4 * half, 1 + 8 * oy:9 + 8 * oy, :, MID] = both.astype(BF16)

    near_own = 8 - 7 * m
    far_own = 1 + 7 * m
    near_margin_there = 9 * m
    near_margin = 9 - 9 * m
    far_margin = 9 * m

    def halo_copies(space, turn):
        copies = []

        def add(src, dst, device):
            at = len(copies)
            copies.append(remote(src, dst, halo_s.at[turn, at], halo_r.at[turn, at], device))

        for j in (2, 1):
            for step, row, landing in ((j, 16, y_low[turn]), (-j, 1, y_high[turn])):
                at = wrap(s + step)
                add(space.at[1:9, row, :, MID], landing.at[j - 1, 1:9], (at, m))
                add(space.at[near_own, row, :, MID], landing.at[j - 1, near_margin_there], (at, other))
        for step, face, landing in ((1, 1, z_low), (-1, 0, z_high)):
            at = wrap(s + step)
            add(faces.at[turn, face], landing.at[turn, 1:9], (at, m))
            add(faces.at[turn, face, near_own - 1], landing.at[turn, near_margin_there], (at, other))
        for step, line, side in ((3, 1, 0), (-3, 0, 1)):
            at = wrap(s + step)
            add(lines.at[turn, line], line_in.at[turn, side, 0], (at, m))
            add(lines.at[turn, line], line_in.at[turn, side, 1], (at, other))
        add(space.at[near_own, 1:17, :, MID], space.at[near_margin_there, 1:17, :, MID], pair)
        beside = len(copies)
        for j in range(1, 8):
            there = (wrap(s + sign * j), other)
            which = slice(1, 3) if j <= 4 else pl.ds(2 * m, 2)
            add(edges.at[turn, which], far_edge[turn].at[j - 1, which], there)
        for j in (2, 1, 3, 4):
            there = (wrap(s + sign * j), other)
            add(space.at[far_own, 1:17, :, MID], far[turn].at[j - 1], there)
        return copies[:beside], copies[beside:]

    def stage(space, turn):
        def one(x, _):
            for face, z in ((0, 0), (1, 15)):
                got = vol.at[x].reshape(256, 128)[pl.ds(z, 16, stride=16), :]
                faces[turn, face, x] = got.astype(BF16)
            return 0

        lax.fori_loop(0, 8, one, 0)
        for line, start in ((0, 0), (1, 255)):
            got = vol.reshape(2048, 128)[pl.ds(start, 8, stride=256), :]
            lines[turn, line] = jnp.concatenate([got, got], axis=0).astype(BF16)
        edges[turn, 0] = space[far_own, 1, :, MID]
        edges[turn, 1] = faces[turn, 0, far_own - 1]
        edges[turn, 2] = faces[turn, 1, far_own - 1]
        edges[turn, 3] = space[far_own, 16, :, MID]

    zero = jnp.zeros((), BF16)

    def beside(k):
        got = near[0, k]
        return got >= 0, got - s

    def shift(space, x, _):
        shift_a[8:296, :] = space[x, :, :, MID].astype(F32).reshape(288, 128)
        for z, start, row in ((0, 7, 0), (1, 9, 15)):
            shift_b[z] = shift_a[start:start + 288, :]
            shift_b.at[z][pl.ds(row, 18, stride=16), :] = margin[z, x]
            lanes = slice(256 * z, 256 * z + 128)
            space[x, :, :, lanes] = shift_b[z].reshape(18, 16, 128).astype(BF16)
        return 0

    def fill_beside(space, turn):
        there, d = beside(15)
        space[:, 17, :, MID] = jnp.where(there, y_high[turn][jnp.clip(d - 1, 0, 1)], zero)
        there, d = beside(10)
        space[:, 0, :, MID] = jnp.where(there, y_low[turn][jnp.clip(-d - 1, 0, 1)], zero)
        there, d = beside(13)
        margin[1, :, 1:17, :] = jnp.where(there, z_high[turn], zero).astype(F32)
        there, d = beside(12)
        margin[0, :, 1:17, :] = jnp.where(there, z_low[turn], zero).astype(F32)
        for k, landing, to, z in ((16, y_high, 17, 1), (14, y_high, 17, 0), (11, y_low, 0, 1), (9, y_low, 0, 0)):
            there, d = beside(k)
            j = jnp.where(d > 0, d, -d)
            row = 0 if z else 15
            got = jnp.where(there, landing[turn][jnp.clip(j - 1, 0, 1)], zero).astype(F32)
            got = got[:, row:row + 1, :]
            margin[z, :, to:to + 1, :] = got
            if k in (16, 9):
                side = 1 if k == 16 else 0
                third = there & (j == 3)
                line = line_in[turn, side, 0].astype(F32)[:8].reshape(8, 1, 128)
                margin[z, 1:9, to:to + 1, :] = jnp.where(third, line, got[1:9])
                beyond = line_in[turn, side, 1].astype(F32)
                beyond = jnp.where(m == 0, beyond[0:1], beyond[7:8])
                margin[z, near_margin, to:to + 1, :] = jnp.where(
                    third, beyond, jnp.where(m == 0, got[9], got[0])
                )
        lax.fori_loop(1 - m, 10 - m, functools.partial(shift, space), 0)

    def fill_far(space, turn):
        for dy in (-1, 0, 1):
            for dz in (-1, 0, 1):
                there, d = beside(17 * m + (dy + 1) * 3 + dz + 1)
                j = sign * d
                slot = jnp.clip(j - 1, 0, 6)
                slot_4 = jnp.clip(j - 1, 0, 3)
                if dy == 0 and dz == 0:
                    space[far_margin, 1:17, :, MID] = jnp.where(there, far[turn][slot_4], zero)
                elif dy == 0:
                    z, edge = (1, 1) if dz == 1 else (0, 2)
                    margin[z, far_margin, 1:17, :] = jnp.where(there, far_edge[turn][slot, edge], zero).astype(F32)
                else:
                    to, edge, at = (17, 0, 0) if dy == 1 else (0, 3, 15)
                    got = jnp.where(j <= 4, far[turn][slot_4, at], far_edge[turn][slot, edge])
                    got = jnp.where(there, got, zero)
                    if dz == 0:
                        space[far_margin, to, :, MID] = got
                    else:
                        z, row = (1, 0) if dz == 1 else (0, 15)
                        margin[z, far_margin, to:to + 1, :] = got.astype(F32)[row:row + 1, :]

        shift(space, far_margin, 0)

    def conv_rows(space, weights, chunk):
        total = None
        for ex in range(3):
            for ey in range(3):
                window = space[pl.ds(2 * chunk + ex, 2), ey:ey + 16].reshape(512, 384)
                tap = ex * 9 + ey * 3
                part = dot(window, weights[tap:tap + 3].reshape(384, 128))
                total = part if total is None else total + part
        return total

    stage(pad, 0)
    copies_beside, copies_far = halo_copies(pad, 0)
    for copy in copies_beside + copies_far:
        copy.start()

    for copy in loads:
        copy.wait()

    def upstream(t, _):
        rows = w_down[pl.ds(pl.multiple_of(t * 256, 256), 256), :]
        got = dot_t(cot[...], rows)
        for z in range(2):
            part = got[:, 128 * z:128 * z + 128].reshape(4, 8, 8, 128)
            for x in range(4):
                up[x, t // 2, :, t % 2, pl.ds(z, 8, stride=2), :] = part[x]
        return 0

    lax.fori_loop(0, 4, upstream, 0)

    def turn_back(tap, _):
        w_back[tap] = w_conv[26 - tap].astype(F32).T.astype(BF16)
        return 0

    lax.fori_loop(0, 27, turn_back, 0)

    for copy in copies_beside:
        copy.wait()
    fill_beside(pad, 0)

    def forward(step, _):
        c = jnp.where(m == 0, 3 - step, step)
        at = pl.ds(2 * c, 2)
        here = mask[at].reshape(512, 128)
        pre = conv_rows(pad, w_conv, c) * here
        sigmoid = 1.0 / (1.0 + jnp.exp(-pre))
        hid[...] = (pre * sigmoid).astype(BF16).astype(F32).reshape(2, 8, 2, 16, 128)
        grad = up[c].reshape(512, 128) * sigmoid * (1.0 + pre * (1.0 - sigmoid)) * here
        grad = grad.astype(BF16)
        grad_wide = grad.astype(F32)
        vol[at] = grad_wide.reshape(2, 16, 16, 128)
        gpad[pl.ds(2 * c + 1, 2), 1:17, :, MID] = grad.reshape(2, 16, 16, 128)
        for x in range(2):
            turned[2 * c + x] = grad_wide[256 * x:256 * x + 256].T.astype(BF16)
        rows = pl.ds(pl.multiple_of(64 * c, 64), 64)
        for tx in range(2):
            for ty in range(2):
                for tz in range(2):
                    t = (tx * 2 + ty) * 2 + tz
                    got = hid[tx, :, ty, pl.ds(tz, 8, stride=2), :].reshape(64, 128)
                    patches[rows, 128 * t:128 * t + 128] = got.astype(BF16)
        return 0

    lax.fori_loop(0, 3, forward, 0)
    for copy in copies_far:
        copy.wait()
    fill_far(pad, 0)
    lax.fori_loop(3, 4, forward, 0)

    stage(gpad, 1)
    grad_beside, grad_far = halo_copies(gpad, 1)
    grad_copies = grad_beside + grad_far
    for copy in grad_copies:
        copy.start()

    for t in range(8):
        got = lax.dot_general(
            patches[:, 128 * t:128 * t + 128], cot[...], (((0,), (0,)), ((), ())), preferred_element_type=F32
        )
        down_st[0, 128 * t:128 * t + 128, :] = got[:, :128]
        down_st[1, 128 * t:128 * t + 128, :] = got[:, 128:]
    down_swap = remote(down_st.at[other], down_in, pair_s.at[1], pair_r.at[1], pair)
    down_swap.start()

    conv_swaps = []
    d1 = []
    for ex in range(3):
        for ey in range(3):
            total = None
            for half in range(2):
                rows = pad[ex + 4 * half:ex + 4 * half + 4, ey:ey + 16].reshape(1024, 384)
                left = jnp.concatenate([turned[4 * half + x] for x in range(4)], axis=1)
                part = dot(left, rows)
                total = part if total is None else total + part
            for ez in range(3):
                tap = total[:, 128 * ez:128 * ez + 128].T
                at = ex * 9 + ey * 3 + ez
                conv_st[0, 64 * at:64 * at + 64, :] = tap[:64]
                conv_st[1, 64 * at:64 * at + 64, :] = tap[64:]
        rows = slice(576 * ex, 576 * ex + 576)
        conv_swaps.append(
            remote(conv_st.at[other, rows], conv_in.at[rows], pair_s.at[3 + ex], pair_r.at[3 + ex], pair)
        )
        conv_swaps[-1].start()
        if ex == 1:
            down_swap.wait()
            down_in[...] = down_in[...] + down_st[m]
            d_bf[...] = down_in[...].reshape(8, 128, 128).astype(BF16)
            for step in range(1, ZS):
                z, device = line_peer(step)
                d1.append(remote(d_bf.at[z], d_in.at[step - 1], d1_s.at[step - 1], d1_r.at[step - 1], device))
                d1[-1].start()
    conv_in[1728:, :] = jnp.zeros((64, 128), F32)
    for ex in range(3):
        rows = slice(576 * ex, 576 * ex + 576)
        conv_swaps[ex].wait()
        conv_in[rows, :] = conv_in[rows, :] + conv_st[m, rows, :]
    c_bf[...] = conv_in[...].reshape(16, 112, 128).astype(BF16)
    c1 = []
    for at, step in enumerate(plane_steps):
        peer, device = plane_peer(step)
        c1.append(remote(c_bf.at[peer], c_in.at[at], c1_s.at[at], c1_r.at[at], device))
        c1[-1].start()

    got = dot(patches[...], w_down[...]).astype(BF16)
    coarse_st[0] = got[:, :128]
    coarse_st[1] = got[:, 128:]
    coarse_swap = remote(coarse_st.at[other], coarse.at[own_half], pair_s.at[2], pair_r.at[2], pair)
    coarse_swap.start()
    coarse_own = pltpu.make_async_copy(coarse_st.at[m], coarse.at[own_half], load.at[4])
    coarse_own.start()

    for copy in d1:
        copy.wait()
    total = down_in[pl.ds(pl.multiple_of(my_z * 128, 128), 128), :]
    for step in range(ZS - 1):
        total = total + d_in[step].astype(F32)
    d_mid[...] = total
    d2 = []
    for at, step in enumerate(plane_steps):
        peer, device = plane_peer(step)
        rows = pl.ds(pl.multiple_of(peer * 8, 8), 8)
        d2.append(remote(d_mid.at[rows], d_in2.at[at], d2_s.at[at], d2_r.at[at], device))
        d2[-1].start()
    for copy in c1:
        copy.wait()
    total = conv_in[pl.ds(pl.multiple_of(plane * 112, 112), 112), :]
    for at in range(15):
        total = total + c_in[at].astype(F32)
    c_line[my_z] = total.astype(BF16)
    c2 = []
    for step in range(1, ZS):
        z, device = line_peer(step)
        c2.append(remote(c_line.at[my_z], c_line.at[my_z], c2_s.at[step - 1], c2_r.at[step - 1], device))
        c2[-1].start()

    for copy in d2:
        copy.wait()
    total = d_mid[pl.ds(pl.multiple_of(plane * 8, 8), 8), :]
    for at in range(15):
        total = total + d_in2[at]
    d_mix[plane] = total
    d4 = []
    for at, step in enumerate(plane_steps):
        peer, device = plane_peer(step)
        d4.append(remote(d_mix.at[plane], d_mix.at[plane], d4_s.at[at], d4_r.at[at], device))
        d4[-1].start()
    for copy in c2:
        copy.wait()
    total = c_line[0].astype(F32)
    for z in range(1, ZS):
        total = total + c_line[z].astype(F32)
    c_tot[...] = total.astype(BF16)
    c3 = []
    for at, step in enumerate(plane_steps):
        peer, device = plane_peer(step)
        c3.append(remote(c_tot, c_out.at[plane], c3_s.at[at], c3_r.at[at], device))
        c3[-1].start()
    c_own = pltpu.make_async_copy(c_tot, c_out.at[plane], load.at[5])
    c_own.start()

    for copy in d4:
        copy.wait()
    d_tot[...] = d_mix[...].reshape(128, 128).astype(BF16)
    d3 = []
    for step in range(1, ZS):
        z, device = line_peer(step)
        d3.append(remote(d_tot, d_out.at[my_z], d3_s.at[step - 1], d3_r.at[step - 1], device))
        d3[-1].start()
    d_own = pltpu.make_async_copy(d_tot, d_out.at[my_z], load.at[6])
    d_own.start()

    for copy in grad_copies:
        copy.wait()
    fill_beside(gpad, 1)
    fill_far(gpad, 1)

    def backward(c, _):
        at = pl.ds(2 * c, 2)
        vol[at] = (conv_rows(gpad, w_back, c) * mask[at].reshape(512, 128)).reshape(2, 16, 16, 128)
        return 0

    lax.fori_loop(0, 4, backward, 0)

    for oy in range(2):
        for oz in range(2):
            got = vol[:, 8 * oy:8 * oy + 8, 8 * oz:8 * oz + 8, :].reshape(512, 128)
            for part in range(2):
                columns = slice(256 * part, 256 * part + 256)
                out_bricks[oy + 2 * oz, :, columns] = got[columns].T.astype(BF16)
    feat_swap = remote(out_bricks.at[:, other_rows, :], g_feat.at[:, m], pair_s.at[6], pair_r.at[6], pair)
    feat_swap.start()
    feat_out = pltpu.make_async_copy(out_bricks.at[:, own_rows, :], g_feat.at[:, m], load.at[7])
    feat_out.start()

    for copy in c3 + d3 + [coarse_swap, feat_swap, coarse_own, c_own, d_own, feat_out]:
        copy.wait()


def hand_on(c_in, d_in, coarse_in, feat_in, g_conv, g_down, coarse, g_feat, c, d, c_wide, d_wide, co, f, sems):
    held = (c, d, co, f)
    moves = [pltpu.make_async_copy(a, b, sems.at[i]) for i, (a, b) in enumerate(zip((c_in, d_in, coarse_in, feat_in), held))]
    for move in moves:
        move.start()

    def out(at, src, dst):
        move = pltpu.make_async_copy(src, dst, sems.at[at])
        move.start()
        return move

    outs = []
    moves[0].wait()
    for part in range(2):
        rows = slice(864 * part, 864 * part + 864)
        c_wide[rows, :] = c[...].reshape(1792, 128)[rows].astype(F32) * (1.0 / BLOCKS)
        outs.append(out(4 + part, c_wide.at[rows], g_conv.at[rows]))
    moves[1].wait()
    d_wide[...] = d[...].reshape(1024, 128).astype(F32) * (1.0 / BLOCKS)
    outs.append(out(6, d_wide, g_down))
    moves[2].wait()
    outs.append(out(7, co, coarse))
    moves[3].wait()
    outs.append(out(8, f, g_feat))
    for move in outs:
        move.wait()


def local(features, heights, neighbours, w_conv, w_down, cotangent):
    anywhere = pl.BlockSpec(memory_space=pl.ANY)
    dma = pltpu.SemaphoreType.DMA
    V = pltpu.VMEM
    scratch = [
        pltpu.SMEM((8, 64), jnp.int32), pltpu.SMEM((1, 26), jnp.int32),
        V((27, 128, 128), BF16), V((1024, 256), BF16), V((256, 256), BF16),
        V((10, 18, 16, 384), BF16),
        V((10, 18, 16, 384), BF16),
        V((8, 16, 16, 128), F32),
        V((4, 2, 8, 2, 16, 128), F32),
        V((8, 16, 16, 128), F32),
        V((4, 128, 512), BF16),
        V((2, 8, 2, 16, 128), F32),
        V((256, 1024), BF16),
        V((8, 128, 256), BF16),
        V((27, 128, 128), BF16),
        V((4, 128, 512), BF16),
        V((304, 128), F32),
        V((2, 288, 128), F32),
        V((2, 10, 18, 128), F32),
        V((2, 2, 8, 16, 128), BF16),
        V((2, 4, 16, 128), BF16),
        V((2, 2, 16, 128), BF16),
        V((2, 10, 16, 128), BF16), V((2, 10, 16, 128), BF16),
        V((2, 10, 16, 128), BF16), V((2, 10, 16, 128), BF16),
        V((2, 10, 16, 128), BF16),
        V((2, 10, 16, 128), BF16),
        V((4, 16, 16, 128), BF16), V((4, 16, 16, 128), BF16),
        V((7, 4, 16, 128), BF16), V((7, 4, 16, 128), BF16),
        V((2, 2, 2, 16, 128), BF16),
        V((2, 256, 128), BF16),
        V((2, 1024, 128), F32),
        V((1024, 128), F32),
        V((2, 1728, 128), F32),
        V((1792, 128), F32),
        V((16, 112, 128), BF16),
        V((15, 112, 128), BF16),
        V((8, 112, 128), BF16),
        V((112, 128), BF16),
        V((8, 128, 128), BF16),
        V((7, 128, 128), BF16),
        V((128, 128), F32), V((15, 8, 128), F32), V((16, 8, 128), F32),
        V((128, 128), BF16),
        dma((10,)), dma((2, 28)), dma((2, 28)), dma((7,)), dma((7,)),
        dma((15,)), dma((15,)), dma((7,)), dma((7,)), dma((15,)), dma((15,)),
        dma((7,)), dma((7,)), dma((15,)), dma((15,)), dma((7,)), dma((7,)), dma((15,)), dma((15,)),
    ]
    made = pl.pallas_call(
        kernel,
        out_shape=(
            jax.ShapeDtypeStruct((512, 128), BF16),
            jax.ShapeDtypeStruct((16, 112, 128), BF16),
            jax.ShapeDtypeStruct((8, 128, 128), BF16),
            jax.ShapeDtypeStruct((4, 2, 64, 512), BF16),
        ),
        in_specs=[anywhere] * 6,
        out_specs=(anywhere,) * 4,
        scratch_shapes=scratch,
        compiler_params=pltpu.CompilerParams(
            collective_id=0, has_side_effects=True, vmem_limit_bytes=58 * 2**20
        ),
        cost_estimate=pl.CostEstimate(
            flops=6_000_000_000, bytes_accessed=6_000_000, transcendentals=262144
        ),
    )(
        heights,
        neighbours,
        features.transpose(0, 2, 1).reshape(4, 2, 64, 512),
        w_conv,
        w_down.reshape(1024, 256),
        cotangent[0],
    )
    coarse, g_conv, g_down, g_feat = made
    g_conv, g_down, coarse, g_feat = pl.pallas_call(
        hand_on,
        out_shape=(
            jax.ShapeDtypeStruct((1728, 128), F32),
            jax.ShapeDtypeStruct((1024, 128), F32),
            jax.ShapeDtypeStruct((512, 128), BF16),
            jax.ShapeDtypeStruct((4, 2, 64, 512), BF16),
        ),
        in_specs=[anywhere] * 4,
        out_specs=(anywhere,) * 4,
        scratch_shapes=[
            V((16, 112, 128), BF16), V((8, 128, 128), BF16), V((1728, 128), F32), V((1024, 128), F32),
            V((512, 128), BF16), V((4, 2, 64, 512), BF16), dma((9,)),
        ],
        compiler_params=pltpu.CompilerParams(vmem_limit_bytes=58 * 2**20),
    )(g_conv, g_down, coarse, g_feat)
    return (
        coarse[None],
        g_conv.reshape(27, 64, 128),
        g_down.reshape(8, 128, 128),
        g_feat.reshape(8, 64, 512).transpose(0, 2, 1),
    )


def solution(mesh):
    placed = (
        P("space", None, "chan"),
        P("space", None),
        P("space", None),
        P(),
        P(),
        P("space", None, None),
    )
    return jax.shard_map(
        local,
        mesh=mesh,
        in_specs=placed,
        out_specs=(
            P("space", None, "chan"),
            P(None, "chan", None),
            P(None, None, "chan"),
            P("space", None, "chan"),
        ),
        check_vma=False,
    )
```

```python
import functools

import jax
import jax.numpy as jnp
from jax import lax
from jax.experimental import pallas as pl
from jax.experimental.pallas import tpu as pltpu
from jax.sharding import PartitionSpec as P

MESH = pl.DeviceIdType.MESH
F32 = jnp.float32
BF16 = jnp.bfloat16
MID = slice(128, 256)
XS, ZS, YS = 4, 8, 4
BLOCKS = XS * ZS * YS


def dot(a, b):
    return jnp.dot(a, b, preferred_element_type=F32)


def dot_t(a, b):
    return lax.dot_general(a, b, (((1,), (1,)), ((), ())), preferred_element_type=F32)


def kernel(
    heights_far, near_far, feat, w_conv_far, w_down_far, cot_far,
    coarse, c_out, d_out, g_feat,
    heights, near, w_conv, w_down, cot,
    pad, gpad, mask, up, vol, cat, hid, patches, turned, w_back, out_bricks,
    shift_a, shift_b, margin,
    faces, edges, lines, y_low_0, y_low_1, y_high_0, y_high_1, z_low, z_high, far_0, far_1, far_edge_0, far_edge_1,
    line_in,
    coarse_st, down_st, down_in, conv_st, conv_in,
    c_bf, c_in, c_line, c_tot, d_bf, d_in, d_mid, d_in2, d_mix, d_tot,
    load, halo_s, halo_r, pair_s, pair_r,
    c1_s, c1_r, c2_s, c2_r, c3_s, c3_r, d1_s, d1_r, d2_s, d2_r, d3_s, d3_r, d4_s, d4_r,
):
    y_low, y_high = (y_low_0, y_low_1), (y_high_0, y_high_1)
    far, far_edge = (far_0, far_1), (far_edge_0, far_edge_1)
    s = lax.axis_index("space")
    m = lax.axis_index("chan")
    other = 1 - m
    sign = 2 * m - 1
    my_y = s % YS
    my_z = s // YS % ZS
    my_x = s // (YS * ZS)
    plane = my_x * YS + my_y
    wrap = lambda index: (index + 2 * BLOCKS) % BLOCKS
    hops = lambda step, size: min(step, size - step)
    plane_steps = [(a, b) for a in range(XS) for b in range(YS) if (a, b) != (0, 0)]
    plane_steps.sort(key=lambda step: -hops(step[0], XS) - hops(step[1], YS))
    line_steps = sorted(range(1, ZS), key=lambda step: -hops(step, ZS))

    def plane_peer(step):
        x, y = (my_x + step[0]) % XS, (my_y + step[1]) % YS
        return x * YS + y, ((x * ZS + my_z) * YS + y, m)

    def line_peer(step):
        z = (my_z + step) % ZS
        return z, ((my_x * ZS + z) * YS + my_y, m)

    def remote(src, dst, send, recv, device):
        return pltpu.make_async_remote_copy(
            src_ref=src, dst_ref=dst, send_sem=send, recv_sem=recv, device_id=device, device_id_type=MESH
        )

    barrier = pltpu.get_barrier_semaphore()
    greeted = [(s, other)]
    for d in (1, 2, 3):
        for e in (d, -d):
            greeted += [(wrap(s + e), m), (wrap(s + e), other)]
    greeted += [(wrap(s + sign * j), other) for j in (4, 5, 6, 7)]
    greeted += [plane_peer(step)[1] for step in plane_steps]
    greeted += [line_peer(step)[1] for step in line_steps]
    for device in greeted:
        pl.semaphore_signal(barrier, inc=1, device_id=device, device_id_type=MESH)

    pair = (s, other)
    own_rows = pl.ds(pl.multiple_of(m * 64, 64), 64)
    other_rows = pl.ds(pl.multiple_of(other * 64, 64), 64)
    own_half = pl.ds(pl.multiple_of(m * 256, 256), 256)
    feat_own = pltpu.make_async_copy(feat.at[:, m], cat.at[:, own_rows, :], load.at[0])
    loads = [
        pltpu.make_async_copy(w_down_far, w_down, load.at[1]),
        pltpu.make_async_copy(cot_far.at[own_half], cot, load.at[2]),
        pltpu.make_async_copy(w_conv_far, w_conv, load.at[3]),
    ]
    scalars = [
        pltpu.make_async_copy(heights_far, heights, load.at[8]),
        pltpu.make_async_copy(near_far, near, load.at[9]),
    ]
    for copy in scalars + [feat_own] + loads:
        copy.start()

    pl.semaphore_wait(barrier, len(greeted))

    swap = remote(feat.at[:, other], cat.at[:, own_rows, :], pair_s.at[0], pair_r.at[0], pair)
    swap.start()
    for copy in scalars:
        copy.wait()
    levels = lax.broadcasted_iota(jnp.int32, (8, 128), 0)

    def mask_plane(x, _):
        for y in range(16):
            for z in range(2):
                height = heights[m + 2 * (y // 8) + 4 * z, x * 8 + y % 8]
                mask[x, y, 8 * z:8 * z + 8, :] = jnp.where(levels < height, 1.0, 0.0)
        return 0

    lax.fori_loop(0, 8, mask_plane, 0)
    feat_own.wait()
    swap.wait()

    for oy in range(2):
        for half in range(2):
            columns = slice(256 * half, 256 * half + 256)
            low = cat[oy, :, columns].astype(F32).T.reshape(4, 8, 8, 128)
            high = cat[oy + 2, :, columns].astype(F32).T.reshape(4, 8, 8, 128)
            both = jnp.concatenate([low, high], axis=2)
            at = slice(4 * half, 4 * half + 4)
            both = both * mask[at, 8 * oy:8 * oy + 8]
            vol[at, 8 * oy:8 * oy + 8] = both
            pad[1 + 4 * half:5 + 4 * half, 1 + 8 * oy:9 + 8 * oy, :, MID] = both.astype(BF16)

    near_own = 8 - 7 * m
    far_own = 1 + 7 * m
    near_margin_there = 9 * m
    near_margin = 9 - 9 * m
    far_margin = 9 * m

    def halo_copies(space, turn):
        copies = []

        def add(src, dst, device):
            at = len(copies)
            copies.append(remote(src, dst, halo_s.at[turn, at], halo_r.at[turn, at], device))

        for j in (2, 1):
            for step, row, landing in ((j, 16, y_low[turn]), (-j, 1, y_high[turn])):
                at = wrap(s + step)
                add(space.at[1:9, row, :, MID], landing.at[j - 1, 1:9], (at, m))
                add(space.at[near_own, row, :, MID], landing.at[j - 1, near_margin_there], (at, other))
        for step, face, landing in ((1, 1, z_low), (-1, 0, z_high)):
            at = wrap(s + step)
            add(faces.at[turn, face], landing.at[turn, 1:9], (at, m))
            add(faces.at[turn, face, near_own - 1], landing.at[turn, near_margin_there], (at, other))
        for step, line, side in ((3, 1, 0), (-3, 0, 1)):
            at = wrap(s + step)
            add(lines.at[turn, line], line_in.at[turn, side, 0], (at, m))
            add(lines.at[turn, line], line_in.at[turn, side, 1], (at, other))
        add(space.at[near_own, 1:17, :, MID], space.at[near_margin_there, 1:17, :, MID], pair)
        beside = len(copies)
        for j in range(1, 8):
            there = (wrap(s + sign * j), other)
            which = slice(1, 3) if j <= 4 else pl.ds(2 * m, 2)
            add(edges.at[turn, which], far_edge[turn].at[j - 1, which], there)
        for j in (2, 1, 3, 4):
            there = (wrap(s + sign * j), other)
            add(space.at[far_own, 1:17, :, MID], far[turn].at[j - 1], there)
        return copies[:beside], copies[beside:]

    def stage(space, turn):
        def one(x, _):
            for face, z in ((0, 0), (1, 15)):
                got = vol.at[x].reshape(256, 128)[pl.ds(z, 16, stride=16), :]
                faces[turn, face, x] = got.astype(BF16)
            return 0

        lax.fori_loop(0, 8, one, 0)
        for line, start in ((0, 0), (1, 255)):
            got = vol.reshape(2048, 128)[pl.ds(start, 8, stride=256), :]
            lines[turn, line] = jnp.concatenate([got, got], axis=0).astype(BF16)
        edges[turn, 0] = space[far_own, 1, :, MID]
        edges[turn, 1] = faces[turn, 0, far_own - 1]
        edges[turn, 2] = faces[turn, 1, far_own - 1]
        edges[turn, 3] = space[far_own, 16, :, MID]

    zero = jnp.zeros((), BF16)

    def beside(k):
        got = near[0, k]
        return got >= 0, got - s

    def shift(space, x, _):
        shift_a[8:296, :] = space[x, :, :, MID].astype(F32).reshape(288, 128)
        for z, start, row in ((0, 7, 0), (1, 9, 15)):
            shift_b[z] = shift_a[start:start + 288, :]
            shift_b.at[z][pl.ds(row, 18, stride=16), :] = margin[z, x]
            lanes = slice(256 * z, 256 * z + 128)
            space[x, :, :, lanes] = shift_b[z].reshape(18, 16, 128).astype(BF16)
        return 0

    def fill_beside(space, turn):
        there, d = beside(15)
        space[:, 17, :, MID] = jnp.where(there, y_high[turn][jnp.clip(d - 1, 0, 1)], zero)
        there, d = beside(10)
        space[:, 0, :, MID] = jnp.where(there, y_low[turn][jnp.clip(-d - 1, 0, 1)], zero)
        there, d = beside(13)
        margin[1, :, 1:17, :] = jnp.where(there, z_high[turn], zero).astype(F32)
        there, d = beside(12)
        margin[0, :, 1:17, :] = jnp.where(there, z_low[turn], zero).astype(F32)
        for k, landing, to, z in ((16, y_high, 17, 1), (14, y_high, 17, 0), (11, y_low, 0, 1), (9, y_low, 0, 0)):
            there, d = beside(k)
            j = jnp.where(d > 0, d, -d)
            row = 0 if z else 15
            got = jnp.where(there, landing[turn][jnp.clip(j - 1, 0, 1)], zero).astype(F32)
            got = got[:, row:row + 1, :]
            margin[z, :, to:to + 1, :] = got
            if k in (16, 9):
                side = 1 if k == 16 else 0
                third = there & (j == 3)
                line = line_in[turn, side, 0].astype(F32)[:8].reshape(8, 1, 128)
                margin[z, 1:9, to:to + 1, :] = jnp.where(third, line, got[1:9])
                beyond = line_in[turn, side, 1].astype(F32)
                beyond = jnp.where(m == 0, beyond[0:1], beyond[7:8])
                margin[z, near_margin, to:to + 1, :] = jnp.where(
                    third, beyond, jnp.where(m == 0, got[9], got[0])
                )
        lax.fori_loop(1 - m, 10 - m, functools.partial(shift, space), 0)

    def fill_far(space, turn):
        for dy in (-1, 0, 1):
            for dz in (-1, 0, 1):
                there, d = beside(17 * m + (dy + 1) * 3 + dz + 1)
                j = sign * d
                slot = jnp.clip(j - 1, 0, 6)
                slot_4 = jnp.clip(j - 1, 0, 3)
                if dy == 0 and dz == 0:
                    space[far_margin, 1:17, :, MID] = jnp.where(there, far[turn][slot_4], zero)
                elif dy == 0:
                    z, edge = (1, 1) if dz == 1 else (0, 2)
                    margin[z, far_margin, 1:17, :] = jnp.where(there, far_edge[turn][slot, edge], zero).astype(F32)
                else:
                    to, edge, at = (17, 0, 0) if dy == 1 else (0, 3, 15)
                    got = jnp.where(j <= 4, far[turn][slot_4, at], far_edge[turn][slot, edge])
                    got = jnp.where(there, got, zero)
                    if dz == 0:
                        space[far_margin, to, :, MID] = got
                    else:
                        z, row = (1, 0) if dz == 1 else (0, 15)
                        margin[z, far_margin, to:to + 1, :] = got.astype(F32)[row:row + 1, :]

        shift(space, far_margin, 0)

    def conv_rows(space, weights, chunk):
        total = None
        for ex in range(3):
            for ey in range(3):
                window = space[pl.ds(2 * chunk + ex, 2), ey:ey + 16].reshape(512, 384)
                tap = ex * 9 + ey * 3
                part = dot(window, weights[tap:tap + 3].reshape(384, 128))
                total = part if total is None else total + part
        return total

    stage(pad, 0)
    copies_beside, copies_far = halo_copies(pad, 0)
    for copy in copies_beside + copies_far:
        copy.start()

    for copy in loads:
        copy.wait()

    def upstream(t, _):
        rows = w_down[pl.ds(pl.multiple_of(t * 256, 256), 256), :]
        got = dot_t(cot[...], rows)
        for z in range(2):
            part = got[:, 128 * z:128 * z + 128].reshape(4, 8, 8, 128)
            for x in range(4):
                up[x, t // 2, :, t % 2, pl.ds(z, 8, stride=2), :] = part[x]
        return 0

    lax.fori_loop(0, 4, upstream, 0)

    def turn_back(tap, _):
        w_back[tap] = w_conv[26 - tap].astype(F32).T.astype(BF16)
        return 0

    lax.fori_loop(0, 27, turn_back, 0)

    for copy in copies_beside:
        copy.wait()
    fill_beside(pad, 0)

    def forward(step, _):
        c = jnp.where(m == 0, 3 - step, step)
        at = pl.ds(2 * c, 2)
        here = mask[at].reshape(512, 128)
        pre = conv_rows(pad, w_conv, c) * here
        sigmoid = 1.0 / (1.0 + jnp.exp(-pre))
        hid[c] = (pre * sigmoid).astype(BF16).astype(F32).reshape(2, 8, 2, 16, 128)
        grad = up[c].reshape(512, 128) * sigmoid * (1.0 + pre * (1.0 - sigmoid)) * here
        grad = grad.astype(BF16)
        grad_wide = grad.astype(F32)
        vol[at] = grad_wide.reshape(2, 16, 16, 128)
        gpad[pl.ds(2 * c + 1, 2), 1:17, :, MID] = grad.reshape(2, 16, 16, 128)
        for x in range(2):
            turned[2 * c + x] = grad_wide[256 * x:256 * x + 256].T.astype(BF16)
        rows = pl.ds(pl.multiple_of(64 * c, 64), 64)
        for tx in range(2):
            for ty in range(2):
                for tz in range(2):
                    t = (tx * 2 + ty) * 2 + tz
                    got = hid[c, tx, :, ty, pl.ds(tz, 8, stride=2), :].reshape(64, 128)
                    patches[rows, 128 * t:128 * t + 128] = got.astype(BF16)
        return 0

    for step in range(3):
        forward(step, 0)
    for copy in copies_far:
        copy.wait()
    fill_far(pad, 0)
    lax.fori_loop(3, 4, forward, 0)

    stage(gpad, 1)
    grad_beside, grad_far = halo_copies(gpad, 1)
    grad_copies = grad_beside + grad_far
    for copy in grad_beside:
        copy.start()

    for t in range(8):
        got = lax.dot_general(
            patches[:, 128 * t:128 * t + 128], cot[...], (((0,), (0,)), ((), ())), preferred_element_type=F32
        )
        down_st[0, 128 * t:128 * t + 128, :] = got[:, :128]
        down_st[1, 128 * t:128 * t + 128, :] = got[:, 128:]
    down_swap = remote(down_st.at[other], down_in, pair_s.at[1], pair_r.at[1], pair)
    down_swap.start()

    conv_swaps = []
    d1 = []
    for ex in range(3):
        total = None
        for part in range(4):
            rows = jnp.concatenate(
                [pad[ex + 2 * part:ex + 2 * part + 2, ey:ey + 16].reshape(512, 384) for ey in range(3)], axis=1
            )
            left = jnp.concatenate([turned[2 * part + x] for x in range(2)], axis=1)
            got = dot(left, rows)
            total = got if total is None else total + got
        for tap in range(9):
            turn = total[:, 128 * tap:128 * tap + 128].T
            at = ex * 9 + tap
            conv_st[0, 64 * at:64 * at + 64, :] = turn[:64]
            conv_st[1, 64 * at:64 * at + 64, :] = turn[64:]
        rows = slice(576 * ex, 576 * ex + 576)
        conv_swaps.append(
            remote(conv_st.at[other, rows], conv_in.at[rows], pair_s.at[3 + ex], pair_r.at[3 + ex], pair)
        )
        conv_swaps[-1].start()
        if ex == 1:
            down_swap.wait()
            down_in[...] = down_in[...] + down_st[m]
            d_bf[...] = down_in[...].reshape(8, 128, 128).astype(BF16)
            for step in line_steps:
                z, device = line_peer(step)
                d1.append(remote(d_bf.at[z], d_in.at[step - 1], d1_s.at[step - 1], d1_r.at[step - 1], device))
                d1[-1].start()
    conv_in[1728:, :] = jnp.zeros((64, 128), F32)
    for ex in range(3):
        rows = slice(576 * ex, 576 * ex + 576)
        conv_swaps[ex].wait()
        conv_in[rows, :] = conv_in[rows, :] + conv_st[m, rows, :]
    c_bf[...] = conv_in[...].reshape(16, 112, 128).astype(BF16)
    c1 = []
    for at, step in enumerate(plane_steps):
        peer, device = plane_peer(step)
        c1.append(remote(c_bf.at[peer], c_in.at[at], c1_s.at[at], c1_r.at[at], device))
        c1[-1].start()

    got = dot(patches[...], w_down[...]).astype(BF16)
    coarse_st[0] = got[:, :128]
    coarse_st[1] = got[:, 128:]
    coarse_swap = remote(coarse_st.at[other], coarse.at[own_half], pair_s.at[2], pair_r.at[2], pair)
    coarse_swap.start()
    coarse_own = pltpu.make_async_copy(coarse_st.at[m], coarse.at[own_half], load.at[4])
    coarse_own.start()

    for copy in d1:
        copy.wait()
    total = down_in[pl.ds(pl.multiple_of(my_z * 128, 128), 128), :]
    for step in range(ZS - 1):
        total = total + d_in[step].astype(F32)
    d_mid[...] = total
    d2 = []
    for at, step in enumerate(plane_steps):
        peer, device = plane_peer(step)
        rows = pl.ds(pl.multiple_of(peer * 8, 8), 8)
        d2.append(remote(d_mid.at[rows], d_in2.at[at], d2_s.at[at], d2_r.at[at], device))
        d2[-1].start()
    for copy in c1:
        copy.wait()
    total = conv_in[pl.ds(pl.multiple_of(plane * 112, 112), 112), :]
    for at in range(15):
        total = total + c_in[at].astype(F32)
    c_line[my_z] = total.astype(BF16)
    c2 = []
    for step in line_steps:
        z, device = line_peer(step)
        c2.append(remote(c_line.at[my_z], c_line.at[my_z], c2_s.at[step - 1], c2_r.at[step - 1], device))
        c2[-1].start()
    for copy in grad_far:
        copy.start()

    for copy in d2:
        copy.wait()
    total = d_mid[pl.ds(pl.multiple_of(plane * 8, 8), 8), :]
    for at in range(15):
        total = total + d_in2[at]
    d_mix[plane] = total
    d4 = []
    for at, step in enumerate(plane_steps):
        peer, device = plane_peer(step)
        d4.append(remote(d_mix.at[plane], d_mix.at[plane], d4_s.at[at], d4_r.at[at], device))
        d4[-1].start()
    for copy in c2:
        copy.wait()
    total = c_line[0].astype(F32)
    for z in range(1, ZS):
        total = total + c_line[z].astype(F32)
    c_tot[...] = total.astype(BF16)
    c3 = []
    for at, step in enumerate(plane_steps):
        peer, device = plane_peer(step)
        c3.append(remote(c_tot, c_out.at[plane], c3_s.at[at], c3_r.at[at], device))
        c3[-1].start()
    c_own = pltpu.make_async_copy(c_tot, c_out.at[plane], load.at[5])
    c_own.start()

    for copy in d4:
        copy.wait()
    d_tot[...] = d_mix[...].reshape(128, 128).astype(BF16)
    d3 = []
    for step in line_steps:
        z, device = line_peer(step)
        d3.append(remote(d_tot, d_out.at[my_z], d3_s.at[step - 1], d3_r.at[step - 1], device))
        d3[-1].start()
    d_own = pltpu.make_async_copy(d_tot, d_out.at[my_z], load.at[6])
    d_own.start()

    for copy in grad_beside:
        copy.wait()
    fill_beside(gpad, 1)

    def backward(step, _):
        c = jnp.where(m == 0, 3 - step, step)
        at = pl.ds(2 * c, 2)
        vol[at] = (conv_rows(gpad, w_back, c) * mask[at].reshape(512, 128)).reshape(2, 16, 16, 128)
        return 0

    lax.fori_loop(0, 3, backward, 0)
    for copy in grad_far:
        copy.wait()
    fill_far(gpad, 1)
    backward(3, 0)

    for oy in range(2):
        for oz in range(2):
            got = vol[:, 8 * oy:8 * oy + 8, 8 * oz:8 * oz + 8, :].reshape(512, 128)
            for part in range(2):
                columns = slice(256 * part, 256 * part + 256)
                out_bricks[oy + 2 * oz, :, columns] = got[columns].T.astype(BF16)
    feat_swap = remote(out_bricks.at[:, other_rows, :], g_feat.at[:, m], pair_s.at[6], pair_r.at[6], pair)
    feat_swap.start()
    feat_out = pltpu.make_async_copy(out_bricks.at[:, own_rows, :], g_feat.at[:, m], load.at[7])
    feat_out.start()

    for copy in c3 + d3 + [coarse_swap, feat_swap, coarse_own, c_own, d_own, feat_out]:
        copy.wait()


def hand_on(c_in, d_in, coarse_in, feat_in, g_conv, g_down, coarse, g_feat, c, d, c_wide, d_wide, co, f, sems):
    held = (c, d, co, f)
    moves = [pltpu.make_async_copy(a, b, sems.at[i]) for i, (a, b) in enumerate(zip((c_in, d_in, coarse_in, feat_in), held))]
    for move in moves:
        move.start()

    def out(at, src, dst):
        move = pltpu.make_async_copy(src, dst, sems.at[at])
        move.start()
        return move

    outs = []
    moves[0].wait()
    for part in range(2):
        rows = slice(864 * part, 864 * part + 864)
        c_wide[rows, :] = c[...].reshape(1792, 128)[rows].astype(F32) * (1.0 / BLOCKS)
        outs.append(out(4 + part, c_wide.at[rows], g_conv.at[rows]))
    moves[1].wait()
    d_wide[...] = d[...].reshape(1024, 128).astype(F32) * (1.0 / BLOCKS)
    outs.append(out(6, d_wide, g_down))
    moves[2].wait()
    outs.append(out(7, co, coarse))
    moves[3].wait()
    outs.append(out(8, f, g_feat))
    for move in outs:
        move.wait()


def local(features, heights, neighbours, w_conv, w_down, cotangent):
    anywhere = pl.BlockSpec(memory_space=pl.ANY)
    dma = pltpu.SemaphoreType.DMA
    V = pltpu.VMEM
    scratch = [
        pltpu.SMEM((8, 64), jnp.int32), pltpu.SMEM((1, 26), jnp.int32),
        V((27, 128, 128), BF16), V((1024, 256), BF16), V((256, 256), BF16),
        V((10, 18, 16, 384), BF16),
        V((10, 18, 16, 384), BF16),
        V((8, 16, 16, 128), F32),
        V((4, 2, 8, 2, 16, 128), F32),
        V((8, 16, 16, 128), F32),
        V((4, 128, 512), BF16),
        V((4, 2, 8, 2, 16, 128), F32),
        V((256, 1024), BF16),
        V((8, 128, 256), BF16),
        V((27, 128, 128), BF16),
        V((4, 128, 512), BF16),
        V((304, 128), F32),
        V((2, 288, 128), F32),
        V((2, 10, 18, 128), F32),
        V((2, 2, 8, 16, 128), BF16),
        V((2, 4, 16, 128), BF16),
        V((2, 2, 16, 128), BF16),
        V((2, 10, 16, 128), BF16), V((2, 10, 16, 128), BF16),
        V((2, 10, 16, 128), BF16), V((2, 10, 16, 128), BF16),
        V((2, 10, 16, 128), BF16),
        V((2, 10, 16, 128), BF16),
        V((4, 16, 16, 128), BF16), V((4, 16, 16, 128), BF16),
        V((7, 4, 16, 128), BF16), V((7, 4, 16, 128), BF16),
        V((2, 2, 2, 16, 128), BF16),
        V((2, 256, 128), BF16),
        V((2, 1024, 128), F32),
        V((1024, 128), F32),
        V((2, 1728, 128), F32),
        V((1792, 128), F32),
        V((16, 112, 128), BF16),
        V((15, 112, 128), BF16),
        V((8, 112, 128), BF16),
        V((112, 128), BF16),
        V((8, 128, 128), BF16),
        V((7, 128, 128), BF16),
        V((128, 128), F32), V((15, 8, 128), F32), V((16, 8, 128), F32),
        V((128, 128), BF16),
        dma((10,)), dma((2, 28)), dma((2, 28)), dma((7,)), dma((7,)),
        dma((15,)), dma((15,)), dma((7,)), dma((7,)), dma((15,)), dma((15,)),
        dma((7,)), dma((7,)), dma((15,)), dma((15,)), dma((7,)), dma((7,)), dma((15,)), dma((15,)),
    ]
    made = pl.pallas_call(
        kernel,
        out_shape=(
            jax.ShapeDtypeStruct((512, 128), BF16),
            jax.ShapeDtypeStruct((16, 112, 128), BF16),
            jax.ShapeDtypeStruct((8, 128, 128), BF16),
            jax.ShapeDtypeStruct((4, 2, 64, 512), BF16),
        ),
        in_specs=[anywhere] * 6,
        out_specs=(anywhere,) * 4,
        scratch_shapes=scratch,
        compiler_params=pltpu.CompilerParams(
            collective_id=0, has_side_effects=True, vmem_limit_bytes=58 * 2**20
        ),
        cost_estimate=pl.CostEstimate(
            flops=6_000_000_000, bytes_accessed=6_000_000, transcendentals=262144
        ),
    )(
        heights,
        neighbours,
        features.transpose(0, 2, 1).reshape(4, 2, 64, 512),
        w_conv,
        w_down.reshape(1024, 256),
        cotangent[0],
    )
    coarse, g_conv, g_down, g_feat = made
    g_conv, g_down, coarse, g_feat = pl.pallas_call(
        hand_on,
        out_shape=(
            jax.ShapeDtypeStruct((1728, 128), F32),
            jax.ShapeDtypeStruct((1024, 128), F32),
            jax.ShapeDtypeStruct((512, 128), BF16),
            jax.ShapeDtypeStruct((4, 2, 64, 512), BF16),
        ),
        in_specs=[anywhere] * 4,
        out_specs=(anywhere,) * 4,
        scratch_shapes=[
            V((16, 112, 128), BF16), V((8, 128, 128), BF16), V((1728, 128), F32), V((1024, 128), F32),
            V((512, 128), BF16), V((4, 2, 64, 512), BF16), dma((9,)),
        ],
        compiler_params=pltpu.CompilerParams(vmem_limit_bytes=58 * 2**20),
    )(g_conv, g_down, coarse, g_feat)
    return (
        coarse[None],
        g_conv.reshape(27, 64, 128),
        g_down.reshape(8, 128, 128),
        g_feat.reshape(8, 64, 512).transpose(0, 2, 1),
    )


def solution(mesh):
    placed = (
        P("space", None, "chan"),
        P("space", None),
        P("space", None),
        P(),
        P(),
        P("space", None, None),
    )
    return jax.shard_map(
        local,
        mesh=mesh,
        in_specs=placed,
        out_specs=(
            P("space", None, "chan"),
            P(None, "chan", None),
            P(None, None, "chan"),
            P("space", None, "chan"),
        ),
        check_vma=False,
    )
```

```python
import functools

import jax
import jax.numpy as jnp
from jax import lax
from jax.experimental import pallas as pl
from jax.experimental.pallas import tpu as pltpu
from jax.sharding import PartitionSpec as P

MESH = pl.DeviceIdType.MESH
F32 = jnp.float32
BF16 = jnp.bfloat16
MID = slice(128, 256)
XS, ZS, YS = 4, 8, 4
BLOCKS = XS * ZS * YS


def dot(a, b):
    return jnp.dot(a, b, preferred_element_type=F32)


def dot_t(a, b):
    return lax.dot_general(a, b, (((1,), (1,)), ((), ())), preferred_element_type=F32)


def kernel(
    heights_far, near_far, feat, w_conv_far, w_down_far, cot_far,
    coarse, c_out, d_out, g_feat,
    heights, near, w_conv, w_down, cot,
    pad, gpad, mask, up, vol, cat, hid, patches, turned, w_back, out_bricks,
    shift_a, shift_b, margin,
    faces, edges, lines, y_low_0, y_low_1, y_high_0, y_high_1, z_low, z_high, far_0, far_1, far_edge_0, far_edge_1,
    line_in,
    coarse_st, down_st, down_in, conv_st, conv_in,
    c_bf, c_in, c_line, c_tot, d_bf, d_in, d_mid, d_in2, d_mix, d_tot,
    load, halo_s, halo_r, pair_s, pair_r,
    c1_s, c1_r, c2_s, c2_r, c3_s, c3_r, d1_s, d1_r, d2_s, d2_r, d3_s, d3_r, d4_s, d4_r,
):
    y_low, y_high = (y_low_0, y_low_1), (y_high_0, y_high_1)
    far, far_edge = (far_0, far_1), (far_edge_0, far_edge_1)
    s = lax.axis_index("space")
    m = lax.axis_index("chan")
    other = 1 - m
    sign = 2 * m - 1
    my_y = s % YS
    my_z = s // YS % ZS
    my_x = s // (YS * ZS)
    plane = my_x * YS + my_y
    wrap = lambda index: (index + 2 * BLOCKS) % BLOCKS
    hops = lambda step, size: min(step, size - step)
    plane_steps = [(a, b) for a in range(XS) for b in range(YS) if (a, b) != (0, 0)]
    plane_steps.sort(key=lambda step: -hops(step[0], XS) - hops(step[1], YS))
    line_steps = sorted(range(1, ZS), key=lambda step: -hops(step, ZS))

    def plane_peer(step):
        x, y = (my_x + step[0]) % XS, (my_y + step[1]) % YS
        return x * YS + y, ((x * ZS + my_z) * YS + y, m)

    def line_peer(step):
        z = (my_z + step) % ZS
        return z, ((my_x * ZS + z) * YS + my_y, m)

    def remote(src, dst, send, recv, device):
        return pltpu.make_async_remote_copy(
            src_ref=src, dst_ref=dst, send_sem=send, recv_sem=recv, device_id=device, device_id_type=MESH
        )

    barrier = pltpu.get_barrier_semaphore()
    greeted = [(s, other)]
    for d in (1, 2, 3):
        for e in (d, -d):
            greeted += [(wrap(s + e), m), (wrap(s + e), other)]
    greeted += [(wrap(s + sign * j), other) for j in (4, 5, 6, 7)]
    greeted += [plane_peer(step)[1] for step in plane_steps]
    greeted += [line_peer(step)[1] for step in line_steps]
    for device in greeted:
        pl.semaphore_signal(barrier, inc=1, device_id=device, device_id_type=MESH)

    pair = (s, other)
    own_rows = pl.ds(pl.multiple_of(m * 64, 64), 64)
    other_rows = pl.ds(pl.multiple_of(other * 64, 64), 64)
    own_half = pl.ds(pl.multiple_of(m * 256, 256), 256)
    feat_own = pltpu.make_async_copy(feat.at[:, m], cat.at[:, own_rows, :], load.at[0])
    loads = [
        pltpu.make_async_copy(w_down_far, w_down, load.at[1]),
        pltpu.make_async_copy(cot_far.at[own_half], cot, load.at[2]),
        pltpu.make_async_copy(w_conv_far, w_conv, load.at[3]),
    ]
    scalars = [
        pltpu.make_async_copy(heights_far, heights, load.at[8]),
        pltpu.make_async_copy(near_far, near, load.at[9]),
    ]
    for copy in scalars + [feat_own] + loads:
        copy.start()

    pl.semaphore_wait(barrier, len(greeted))

    swap = remote(feat.at[:, other], cat.at[:, own_rows, :], pair_s.at[0], pair_r.at[0], pair)
    swap.start()
    for copy in scalars:
        copy.wait()
    levels = lax.broadcasted_iota(jnp.int32, (8, 128), 0)

    def mask_plane(x, _):
        for y in range(16):
            for z in range(2):
                height = heights[m + 2 * (y // 8) + 4 * z, x * 8 + y % 8]
                mask[x, y, 8 * z:8 * z + 8, :] = jnp.where(levels < height, 1.0, 0.0)
        return 0

    lax.fori_loop(0, 8, mask_plane, 0)
    feat_own.wait()
    swap.wait()

    for oy in range(2):
        for half in range(2):
            columns = slice(256 * half, 256 * half + 256)
            low = cat[oy, :, columns].astype(F32).T.reshape(4, 8, 8, 128)
            high = cat[oy + 2, :, columns].astype(F32).T.reshape(4, 8, 8, 128)
            both = jnp.concatenate([low, high], axis=2)
            at = slice(4 * half, 4 * half + 4)
            both = both * mask[at, 8 * oy:8 * oy + 8]
            vol[at, 8 * oy:8 * oy + 8] = both
            pad[1 + 4 * half:5 + 4 * half, 1 + 8 * oy:9 + 8 * oy, :, MID] = both.astype(BF16)

    near_own = 8 - 7 * m
    far_own = 1 + 7 * m
    near_margin_there = 9 * m
    near_margin = 9 - 9 * m
    far_margin = 9 * m

    def halo_copies(space, turn):
        copies = []

        def add(src, dst, device):
            at = len(copies)
            copies.append(remote(src, dst, halo_s.at[turn, at], halo_r.at[turn, at], device))

        for j in (2, 1):
            for step, row, landing in ((j, 16, y_low[turn]), (-j, 1, y_high[turn])):
                at = wrap(s + step)
                add(space.at[1:9, row, :, MID], landing.at[j - 1, 1:9], (at, m))
                add(space.at[near_own, row, :, MID], landing.at[j - 1, near_margin_there], (at, other))
        for step, face, landing in ((1, 1, z_low), (-1, 0, z_high)):
            at = wrap(s + step)
            add(faces.at[turn, face], landing.at[turn, 1:9], (at, m))
            add(faces.at[turn, face, near_own - 1], landing.at[turn, near_margin_there], (at, other))
        for step, line, side in ((3, 1, 0), (-3, 0, 1)):
            at = wrap(s + step)
            add(lines.at[turn, line], line_in.at[turn, side, 0], (at, m))
            add(lines.at[turn, line], line_in.at[turn, side, 1], (at, other))
        add(space.at[near_own, 1:17, :, MID], space.at[near_margin_there, 1:17, :, MID], pair)
        beside = len(copies)
        for j in range(1, 8):
            there = (wrap(s + sign * j), other)
            which = slice(1, 3) if j <= 4 else pl.ds(2 * m, 2)
            add(edges.at[turn, which], far_edge[turn].at[j - 1, which], there)
        for j in (2, 1, 3, 4):
            there = (wrap(s + sign * j), other)
            add(space.at[far_own, 1:17, :, MID], far[turn].at[j - 1], there)
        return copies[:beside], copies[beside:]

    def stage(space, turn):
        def one(x, _):
            for face, z in ((0, 0), (1, 15)):
                got = vol.at[x].reshape(256, 128)[pl.ds(z, 16, stride=16), :]
                faces[turn, face, x] = got.astype(BF16)
            return 0

        lax.fori_loop(0, 8, one, 0)
        for line, start in ((0, 0), (1, 255)):
            got = vol.reshape(2048, 128)[pl.ds(start, 8, stride=256), :]
            lines[turn, line] = jnp.concatenate([got, got], axis=0).astype(BF16)
        edges[turn, 0] = space[far_own, 1, :, MID]
        edges[turn, 1] = faces[turn, 0, far_own - 1]
        edges[turn, 2] = faces[turn, 1, far_own - 1]
        edges[turn, 3] = space[far_own, 16, :, MID]

    zero = jnp.zeros((), BF16)

    def beside(k):
        got = near[0, k]
        return got >= 0, got - s

    def shift(space, x, _):
        shift_a[8:296, :] = space[x, :, :, MID].astype(F32).reshape(288, 128)
        for z, start, row in ((0, 7, 0), (1, 9, 15)):
            shift_b[z] = shift_a[start:start + 288, :]
            shift_b.at[z][pl.ds(row, 18, stride=16), :] = margin[z, x]
            lanes = slice(256 * z, 256 * z + 128)
            space[x, :, :, lanes] = shift_b[z].reshape(18, 16, 128).astype(BF16)
        return 0

    def fill_beside(space, turn):
        there, d = beside(15)
        space[:, 17, :, MID] = jnp.where(there, y_high[turn][jnp.clip(d - 1, 0, 1)], zero)
        there, d = beside(10)
        space[:, 0, :, MID] = jnp.where(there, y_low[turn][jnp.clip(-d - 1, 0, 1)], zero)
        there, d = beside(13)
        margin[1, :, 1:17, :] = jnp.where(there, z_high[turn], zero).astype(F32)
        there, d = beside(12)
        margin[0, :, 1:17, :] = jnp.where(there, z_low[turn], zero).astype(F32)
        for k, landing, to, z in ((16, y_high, 17, 1), (14, y_high, 17, 0), (11, y_low, 0, 1), (9, y_low, 0, 0)):
            there, d = beside(k)
            j = jnp.where(d > 0, d, -d)
            row = 0 if z else 15
            got = jnp.where(there, landing[turn][jnp.clip(j - 1, 0, 1)], zero).astype(F32)
            got = got[:, row:row + 1, :]
            margin[z, :, to:to + 1, :] = got
            if k in (16, 9):
                side = 1 if k == 16 else 0
                third = there & (j == 3)
                line = line_in[turn, side, 0].astype(F32)[:8].reshape(8, 1, 128)
                margin[z, 1:9, to:to + 1, :] = jnp.where(third, line, got[1:9])
                beyond = line_in[turn, side, 1].astype(F32)
                beyond = jnp.where(m == 0, beyond[0:1], beyond[7:8])
                margin[z, near_margin, to:to + 1, :] = jnp.where(
                    third, beyond, jnp.where(m == 0, got[9], got[0])
                )
        lax.fori_loop(1 - m, 10 - m, functools.partial(shift, space), 0)

    def fill_far(space, turn):
        for dy in (-1, 0, 1):
            for dz in (-1, 0, 1):
                there, d = beside(17 * m + (dy + 1) * 3 + dz + 1)
                j = sign * d
                slot = jnp.clip(j - 1, 0, 6)
                slot_4 = jnp.clip(j - 1, 0, 3)
                if dy == 0 and dz == 0:
                    space[far_margin, 1:17, :, MID] = jnp.where(there, far[turn][slot_4], zero)
                elif dy == 0:
                    z, edge = (1, 1) if dz == 1 else (0, 2)
                    margin[z, far_margin, 1:17, :] = jnp.where(there, far_edge[turn][slot, edge], zero).astype(F32)
                else:
                    to, edge, at = (17, 0, 0) if dy == 1 else (0, 3, 15)
                    got = jnp.where(j <= 4, far[turn][slot_4, at], far_edge[turn][slot, edge])
                    got = jnp.where(there, got, zero)
                    if dz == 0:
                        space[far_margin, to, :, MID] = got
                    else:
                        z, row = (1, 0) if dz == 1 else (0, 15)
                        margin[z, far_margin, to:to + 1, :] = got.astype(F32)[row:row + 1, :]

        shift(space, far_margin, 0)

    def conv_rows(space, weights, chunk):
        total = None
        for ex in range(3):
            for ey in range(3):
                window = space[pl.ds(2 * chunk + ex, 2), ey:ey + 16].reshape(512, 384)
                tap = ex * 9 + ey * 3
                part = dot(window, weights[tap:tap + 3].reshape(384, 128))
                total = part if total is None else total + part
        return total

    stage(pad, 0)
    copies_beside, copies_far = halo_copies(pad, 0)
    for copy in copies_beside + copies_far:
        copy.start()

    for copy in loads:
        copy.wait()

    def upstream(t, _):
        rows = w_down[pl.ds(pl.multiple_of(t * 256, 256), 256), :]
        got = dot_t(cot[...], rows)
        for z in range(2):
            part = got[:, 128 * z:128 * z + 128].reshape(4, 8, 8, 128)
            for x in range(4):
                up[x, t // 2, :, t % 2, pl.ds(z, 8, stride=2), :] = part[x]
        return 0

    lax.fori_loop(0, 4, upstream, 0)

    def turn_back(tap, _):
        w_back[tap] = w_conv[26 - tap].astype(F32).T.astype(BF16)
        return 0

    lax.fori_loop(0, 27, turn_back, 0)

    for copy in copies_beside:
        copy.wait()
    fill_beside(pad, 0)

    def forward(step, _):
        c = jnp.where(m == 0, 3 - step, step)
        at = pl.ds(2 * c, 2)
        here = mask[at].reshape(512, 128)
        pre = conv_rows(pad, w_conv, c) * here
        sigmoid = 1.0 / (1.0 + jnp.exp(-pre))
        hid[c] = (pre * sigmoid).astype(BF16).astype(F32).reshape(2, 8, 2, 16, 128)
        grad = up[c].reshape(512, 128) * sigmoid * (1.0 + pre * (1.0 - sigmoid)) * here
        grad = grad.astype(BF16)
        grad_wide = grad.astype(F32)
        vol[at] = grad_wide.reshape(2, 16, 16, 128)
        gpad[pl.ds(2 * c + 1, 2), 1:17, :, MID] = grad.reshape(2, 16, 16, 128)
        for x in range(2):
            turned[2 * c + x] = grad_wide[256 * x:256 * x + 256].T.astype(BF16)
        rows = pl.ds(pl.multiple_of(64 * c, 64), 64)
        for tx in range(2):
            for ty in range(2):
                for tz in range(2):
                    t = (tx * 2 + ty) * 2 + tz
                    got = hid[c, tx, :, ty, pl.ds(tz, 8, stride=2), :].reshape(64, 128)
                    patches[rows, 128 * t:128 * t + 128] = got.astype(BF16)
        return 0

    for step in range(3):
        forward(step, 0)
    for copy in copies_far:
        copy.wait()
    fill_far(pad, 0)
    lax.fori_loop(3, 4, forward, 0)

    stage(gpad, 1)
    grad_beside, grad_far = halo_copies(gpad, 1)
    grad_copies = grad_beside + grad_far
    for copy in grad_beside:
        copy.start()

    for t in range(8):
        got = lax.dot_general(
            patches[:, 128 * t:128 * t + 128], cot[...], (((0,), (0,)), ((), ())), preferred_element_type=F32
        )
        down_st[0, 128 * t:128 * t + 128, :] = got[:, :128]
        down_st[1, 128 * t:128 * t + 128, :] = got[:, 128:]
    down_swap = remote(down_st.at[other], down_in, pair_s.at[1], pair_r.at[1], pair)
    down_swap.start()

    conv_swaps = []
    d1 = []
    for ex in range(3):
        total = None
        for part in range(4):
            rows = jnp.concatenate(
                [pad[ex + 2 * part:ex + 2 * part + 2, ey:ey + 16].reshape(512, 384) for ey in range(3)], axis=1
            )
            left = jnp.concatenate([turned[2 * part + x] for x in range(2)], axis=1)
            got = dot(left, rows)
            total = got if total is None else total + got
        for tap in range(9):
            turn = total[:, 128 * tap:128 * tap + 128].T
            at = ex * 9 + tap
            conv_st[0, 64 * at:64 * at + 64, :] = turn[:64]
            conv_st[1, 64 * at:64 * at + 64, :] = turn[64:]
        rows = slice(576 * ex, 576 * ex + 576)
        conv_swaps.append(
            remote(conv_st.at[other, rows], conv_in.at[rows], pair_s.at[3 + ex], pair_r.at[3 + ex], pair)
        )
        conv_swaps[-1].start()
        if ex == 1:
            down_swap.wait()
            down_in[...] = down_in[...] + down_st[m]
            d_bf[...] = down_in[...].reshape(8, 128, 128).astype(BF16)
            for step in line_steps:
                z, device = line_peer(step)
                d1.append(remote(d_bf.at[z], d_in.at[step - 1], d1_s.at[step - 1], d1_r.at[step - 1], device))
                d1[-1].start()
    conv_in[1728:, :] = jnp.zeros((64, 128), F32)
    for ex in range(3):
        rows = slice(576 * ex, 576 * ex + 576)
        conv_swaps[ex].wait()
        conv_in[rows, :] = conv_in[rows, :] + conv_st[m, rows, :]
    c_bf[...] = conv_in[...].reshape(16, 112, 128).astype(BF16)
    c1 = []
    for at, step in enumerate(plane_steps):
        peer, device = plane_peer(step)
        c1.append(remote(c_bf.at[peer], c_in.at[at], c1_s.at[at], c1_r.at[at], device))
        c1[-1].start()

    got = dot(patches[...], w_down[...]).astype(BF16)
    coarse_st[0] = got[:, :128]
    coarse_st[1] = got[:, 128:]
    coarse_swap = remote(coarse_st.at[other], coarse.at[own_half], pair_s.at[2], pair_r.at[2], pair)
    coarse_swap.start()
    coarse_own = pltpu.make_async_copy(coarse_st.at[m], coarse.at[own_half], load.at[4])
    coarse_own.start()

    for copy in c1:
        copy.wait()
    total = conv_in[pl.ds(pl.multiple_of(plane * 112, 112), 112), :]
    for at in range(15):
        total = total + c_in[at].astype(F32)
    c_line[my_z] = total.astype(BF16)
    c2 = []
    for step in line_steps:
        z, device = line_peer(step)
        c2.append(remote(c_line.at[my_z], c_line.at[my_z], c2_s.at[step - 1], c2_r.at[step - 1], device))
        c2[-1].start()
    for copy in grad_far:
        copy.start()

    for copy in d1:
        copy.wait()
    total = down_in[pl.ds(pl.multiple_of(my_z * 128, 128), 128), :]
    for step in range(ZS - 1):
        total = total + d_in[step].astype(F32)
    d_mid[...] = total
    d2 = []
    for at, step in enumerate(plane_steps):
        peer, device = plane_peer(step)
        rows = pl.ds(pl.multiple_of(peer * 8, 8), 8)
        d2.append(remote(d_mid.at[rows], d_in2.at[at], d2_s.at[at], d2_r.at[at], device))
        d2[-1].start()
    for copy in d2:
        copy.wait()
    total = d_mid[pl.ds(pl.multiple_of(plane * 8, 8), 8), :]
    for at in range(15):
        total = total + d_in2[at]
    d_mix[plane] = total
    d4 = []
    for at, step in enumerate(plane_steps):
        peer, device = plane_peer(step)
        d4.append(remote(d_mix.at[plane], d_mix.at[plane], d4_s.at[at], d4_r.at[at], device))
        d4[-1].start()
    for copy in c2:
        copy.wait()
    total = c_line[0].astype(F32)
    for z in range(1, ZS):
        total = total + c_line[z].astype(F32)
    c_tot[...] = total.astype(BF16)
    c3 = []
    for at, step in enumerate(plane_steps):
        peer, device = plane_peer(step)
        c3.append(remote(c_tot, c_out.at[plane], c3_s.at[at], c3_r.at[at], device))
        c3[-1].start()
    c_own = pltpu.make_async_copy(c_tot, c_out.at[plane], load.at[5])
    c_own.start()

    for copy in d4:
        copy.wait()
    d_tot[...] = d_mix[...].reshape(128, 128).astype(BF16)
    d3 = []
    for step in line_steps:
        z, device = line_peer(step)
        d3.append(remote(d_tot, d_out.at[my_z], d3_s.at[step - 1], d3_r.at[step - 1], device))
        d3[-1].start()
    d_own = pltpu.make_async_copy(d_tot, d_out.at[my_z], load.at[6])
    d_own.start()

    for copy in grad_beside:
        copy.wait()
    fill_beside(gpad, 1)

    def backward(step, _):
        c = jnp.where(m == 0, 3 - step, step)
        at = pl.ds(2 * c, 2)
        vol[at] = (conv_rows(gpad, w_back, c) * mask[at].reshape(512, 128)).reshape(2, 16, 16, 128)
        return 0

    lax.fori_loop(0, 3, backward, 0)
    for copy in grad_far:
        copy.wait()
    fill_far(gpad, 1)
    backward(3, 0)

    for oy in range(2):
        for oz in range(2):
            got = vol[:, 8 * oy:8 * oy + 8, 8 * oz:8 * oz + 8, :].reshape(512, 128)
            for part in range(2):
                columns = slice(256 * part, 256 * part + 256)
                out_bricks[oy + 2 * oz, :, columns] = got[columns].T.astype(BF16)
    feat_swap = remote(out_bricks.at[:, other_rows, :], g_feat.at[:, m], pair_s.at[6], pair_r.at[6], pair)
    feat_swap.start()
    feat_out = pltpu.make_async_copy(out_bricks.at[:, own_rows, :], g_feat.at[:, m], load.at[7])
    feat_out.start()

    for copy in c3 + d3 + [coarse_swap, feat_swap, coarse_own, c_own, d_own, feat_out]:
        copy.wait()


def hand_on(c_in, d_in, coarse_in, feat_in, g_conv, g_down, coarse, g_feat, c, d, c_wide, d_wide, co, f, sems):
    held = (c, d, co, f)
    moves = [pltpu.make_async_copy(a, b, sems.at[i]) for i, (a, b) in enumerate(zip((c_in, d_in, coarse_in, feat_in), held))]
    for move in moves:
        move.start()

    def out(at, src, dst):
        move = pltpu.make_async_copy(src, dst, sems.at[at])
        move.start()
        return move

    outs = []
    moves[0].wait()
    for part in range(2):
        rows = slice(864 * part, 864 * part + 864)
        c_wide[rows, :] = c[...].reshape(1792, 128)[rows].astype(F32) * (1.0 / BLOCKS)
        outs.append(out(4 + part, c_wide.at[rows], g_conv.at[rows]))
    moves[1].wait()
    d_wide[...] = d[...].reshape(1024, 128).astype(F32) * (1.0 / BLOCKS)
    outs.append(out(6, d_wide, g_down))
    moves[2].wait()
    outs.append(out(7, co, coarse))
    moves[3].wait()
    outs.append(out(8, f, g_feat))
    for move in outs:
        move.wait()


def local(features, heights, neighbours, w_conv, w_down, cotangent):
    anywhere = pl.BlockSpec(memory_space=pl.ANY)
    dma = pltpu.SemaphoreType.DMA
    V = pltpu.VMEM
    scratch = [
        pltpu.SMEM((8, 64), jnp.int32), pltpu.SMEM((1, 26), jnp.int32),
        V((27, 128, 128), BF16), V((1024, 256), BF16), V((256, 256), BF16),
        V((10, 18, 16, 384), BF16),
        V((10, 18, 16, 384), BF16),
        V((8, 16, 16, 128), F32),
        V((4, 2, 8, 2, 16, 128), F32),
        V((8, 16, 16, 128), F32),
        V((4, 128, 512), BF16),
        V((4, 2, 8, 2, 16, 128), F32),
        V((256, 1024), BF16),
        V((8, 128, 256), BF16),
        V((27, 128, 128), BF16),
        V((4, 128, 512), BF16),
        V((304, 128), F32),
        V((2, 288, 128), F32),
        V((2, 10, 18, 128), F32),
        V((2, 2, 8, 16, 128), BF16),
        V((2, 4, 16, 128), BF16),
        V((2, 2, 16, 128), BF16),
        V((2, 10, 16, 128), BF16), V((2, 10, 16, 128), BF16),
        V((2, 10, 16, 128), BF16), V((2, 10, 16, 128), BF16),
        V((2, 10, 16, 128), BF16),
        V((2, 10, 16, 128), BF16),
        V((4, 16, 16, 128), BF16), V((4, 16, 16, 128), BF16),
        V((7, 4, 16, 128), BF16), V((7, 4, 16, 128), BF16),
        V((2, 2, 2, 16, 128), BF16),
        V((2, 256, 128), BF16),
        V((2, 1024, 128), F32),
        V((1024, 128), F32),
        V((2, 1728, 128), F32),
        V((1792, 128), F32),
        V((16, 112, 128), BF16),
        V((15, 112, 128), BF16),
        V((8, 112, 128), BF16),
        V((112, 128), BF16),
        V((8, 128, 128), BF16),
        V((7, 128, 128), BF16),
        V((128, 128), F32), V((15, 8, 128), F32), V((16, 8, 128), F32),
        V((128, 128), BF16),
        dma((10,)), dma((2, 28)), dma((2, 28)), dma((7,)), dma((7,)),
        dma((15,)), dma((15,)), dma((7,)), dma((7,)), dma((15,)), dma((15,)),
        dma((7,)), dma((7,)), dma((15,)), dma((15,)), dma((7,)), dma((7,)), dma((15,)), dma((15,)),
    ]
    made = pl.pallas_call(
        kernel,
        out_shape=(
            jax.ShapeDtypeStruct((512, 128), BF16),
            jax.ShapeDtypeStruct((16, 112, 128), BF16),
            jax.ShapeDtypeStruct((8, 128, 128), BF16),
            jax.ShapeDtypeStruct((4, 2, 64, 512), BF16),
        ),
        in_specs=[anywhere] * 6,
        out_specs=(anywhere,) * 4,
        scratch_shapes=scratch,
        compiler_params=pltpu.CompilerParams(
            collective_id=0, has_side_effects=True, vmem_limit_bytes=58 * 2**20
        ),
        cost_estimate=pl.CostEstimate(
            flops=6_000_000_000, bytes_accessed=6_000_000, transcendentals=262144
        ),
    )(
        heights,
        neighbours,
        features.transpose(0, 2, 1).reshape(4, 2, 64, 512),
        w_conv,
        w_down.reshape(1024, 256),
        cotangent[0],
    )
    coarse, g_conv, g_down, g_feat = made
    g_conv, g_down, coarse, g_feat = pl.pallas_call(
        hand_on,
        out_shape=(
            jax.ShapeDtypeStruct((1728, 128), F32),
            jax.ShapeDtypeStruct((1024, 128), F32),
            jax.ShapeDtypeStruct((512, 128), BF16),
            jax.ShapeDtypeStruct((4, 2, 64, 512), BF16),
        ),
        in_specs=[anywhere] * 4,
        out_specs=(anywhere,) * 4,
        scratch_shapes=[
            V((16, 112, 128), BF16), V((8, 128, 128), BF16), V((1728, 128), F32), V((1024, 128), F32),
            V((512, 128), BF16), V((4, 2, 64, 512), BF16), dma((9,)),
        ],
        compiler_params=pltpu.CompilerParams(vmem_limit_bytes=58 * 2**20),
    )(g_conv, g_down, coarse, g_feat)
    return (
        coarse[None],
        g_conv.reshape(27, 64, 128),
        g_down.reshape(8, 128, 128),
        g_feat.reshape(8, 64, 512).transpose(0, 2, 1),
    )


def solution(mesh):
    placed = (
        P("space", None, "chan"),
        P("space", None),
        P("space", None),
        P(),
        P(),
        P("space", None, None),
    )
    return jax.shard_map(
        local,
        mesh=mesh,
        in_specs=placed,
        out_specs=(
            P("space", None, "chan"),
            P(None, "chan", None),
            P(None, None, "chan"),
            P("space", None, "chan"),
        ),
        check_vma=False,
    )
```
